32 devices in a mesh: row: 4 (over y, x), col: 8 (over z, core).
Axes of the slice: x: 2, y: 2, z: 4, core: 2. Of those that a mesh axis runs over, the one named last changes fastest.
Arguments:
- trail_grad: float32 [16384, 16384], P('row', 'col'), may hold values from -20 to 20, as said below
- factor_rows: float32 [16384, 768], P('col', 'row'), may hold values from -0.046875 to 0.046875
- factor_top: float32 [768, 768], replicated, may hold values from -1 to 2, as said below
- rows_grad: float32 [16384, 768], P(('row', 'col')), may hold values from -6 to 6
- top_grad: float32 [768, 768], replicated, may hold values from -6 to 6, as said below
Outputs:
- rows_adjoint: float32 [16384, 768], P(('row', 'col'))
- top_adjoint: float32 [768, 768], replicated
The draws below stay inside these ranges and needn't reach their ends.
Inputs may be any that keep to these rules, and one draw needn't show every extreme that they name: trail_grad is symmetric once both of its orders are reverted. factor_top is lower triangular with its diagonal between 1 and 2. top_grad is lower triangular.
All inputs are finite; a program needn't handle non-finite values.
Results may differ from the reference program's by a relative error of at most 0.0001.
Values sent between devices are 32-bit elements; how exact they have to be, the bound alone decides.
No kernel may reach another device: no remote copies, remote signals or barrier semaphores. Data moves between devices by JAX's collectives and lax.ppermute only.
A program may use at most 128 MiB of HBM per device.

```python
import jax
import jax.numpy as jnp
from jax import lax

M = 16384
NB = 256
NP = 3
CB = 128
PW = 768
N_ROW = 4
N_COL = 8


def stored_order_drawn(matrix, owners):
    tile_count = matrix.shape[0] // (owners * CB)
    return matrix.reshape(tile_count, owners, CB, matrix.shape[1]).transpose(1, 0, 2, 3).reshape(matrix.shape)


def draw_trail_grad(key, part):
    first = jax.random.fold_in(jax.random.fold_in(key, 11), 0)
    base = jnp.clip(jax.random.normal(first, (M, M), jnp.float32), -6.0, 6.0)
    symmetric = (base + base.T) * 0.35355339
    rows_done = stored_order_drawn(symmetric, N_ROW)
    return stored_order_drawn(rows_done.T, N_COL).T


def draw_factor_top(key, part):
    first, second = jax.random.split(jax.random.fold_in(key, 23))
    panel_width = NP * NB
    row_ids = lax.broadcasted_iota(jnp.int32, (panel_width, panel_width), 0)
    col_ids = lax.broadcasted_iota(jnp.int32, (panel_width, panel_width), 1)
    noise = jnp.clip(jax.random.normal(first, (panel_width, panel_width), jnp.float32), -4.0, 4.0)
    diag_values = jax.random.uniform(second, (panel_width, panel_width), jnp.float32, 1.0, 2.0)
    same_panel = row_ids // NB == col_ids // NB
    lower_part = jnp.where(same_panel, 0.45 * noise, noise) / jnp.sqrt(jnp.float32(NB))
    lower_part = jnp.clip(lower_part, -1.0, 1.0)
    return jnp.where(row_ids == col_ids, diag_values, jnp.where(row_ids > col_ids, lower_part, 0.0))


def draw_top_grad(key, part):
    first = jax.random.fold_in(key, 37)
    panel_width = NP * NB
    values = jnp.clip(jax.random.normal(first, (panel_width, panel_width), jnp.float32), -6.0, 6.0)
    return jnp.tril(values)


def shard_levels(own_key, extent, cuts, least, high):
    def one(axis_at, shards_of):
        heights = jax.random.uniform(jax.random.fold_in(jax.random.fold_in(own_key, 6), axis_at), (shards_of,), jnp.float32, least / len(cuts), high / len(cuts))
        return jnp.repeat(jnp.exp(heights), extent[axis_at] // shards_of).reshape((-1,) + (1,) * (len(extent) - axis_at - 1))

    level = one(*cuts[0])
    for cut in cuts[1:]:
        level = level * one(*cut)
    return level


def bell_draw(key, shape, scale, reach, pieces=(), kind=jnp.bfloat16):
    result = jax.random.normal(key, shape, jnp.float32) * scale
    if len(pieces) > 0:
        result = shard_levels(key, shape, pieces, -0.22, 0.18) * result
    return jnp.clip(result, min=-reach, max=reach).astype(kind)


def setup_inputs(seed: int = 0) -> dict:
    splits = jax.random.split(jax.random.key(seed), 6)
    return {
        "trail_grad": draw_trail_grad(jax.random.fold_in(splits[5], 71), 0),
        "factor_rows": bell_draw(splits[1], (M, PW), M ** -0.5, 0.046875, ((0, 8), (1, 4)), jnp.float32),
        "factor_top": draw_factor_top(jax.random.fold_in(splits[5], 71), 0),
        "rows_grad": bell_draw(splits[3], (M, PW), 1.0, 6.0, ((0, 32),), jnp.float32),
        "top_grad": draw_top_grad(jax.random.fold_in(splits[5], 71), 0),
    }


exact_dots = lax.Precision.HIGHEST

def natural_order(stored, owners):
    tile_count = stored.shape[0] // (owners * CB)
    return stored.reshape(owners, tile_count, CB, stored.shape[1]).transpose(1, 0, 2, 3).reshape(stored.shape)

def stored_order(matrix, owners):
    tile_count = matrix.shape[0] // (owners * CB)
    return matrix.reshape(tile_count, owners, CB, matrix.shape[1]).transpose(1, 0, 2, 3).reshape(matrix.shape)

def product(left, right):
    return jnp.dot(left.astype(jnp.float32), right.astype(jnp.float32), precision=exact_dots, preferred_element_type=jnp.float32)

def halve_diagonal(matrix):
    order = matrix.shape[0]
    row_ids = lax.broadcasted_iota(jnp.int32, (order, order), 0)
    col_ids = lax.broadcasted_iota(jnp.int32, (order, order), 1)
    return jnp.where(row_ids > col_ids, matrix, jnp.where(row_ids == col_ids, 0.5 * matrix, 0.0))

def cholesky_adjoint(factor, inverse, gradient):
    inner = halve_diagonal(product(factor.T, gradient))
    middle = product(product(inverse.T, inner), inverse)
    return halve_diagonal(middle + middle.T)

def reference(trail_grad, factor_rows, factor_top, rows_grad, top_grad):
    panel_width = NP * NB
    twice = 2.0 * product(trail_grad, factor_rows)
    trail_part = natural_order(twice, N_ROW)
    factor_nat = natural_order(factor_rows, N_COL)
    grad_nat = natural_order(rows_grad, N_ROW)
    row_index = lax.broadcasted_iota(jnp.int32, (panel_width, NB), 0)
    identity = jnp.eye(NB, dtype=jnp.float32)
    adj_rows = jnp.zeros((M, panel_width), jnp.float32)
    adj_top = jnp.zeros((panel_width, panel_width), jnp.float32)
    for which_panel in reversed(range(NP)):
        col_start = which_panel * NB
        col_end = col_start + NB
        below_diag = jnp.where(row_index >= col_end, factor_top[:, col_start:col_end], 0.0)
        diag_block = factor_top[col_start:col_end, col_start:col_end]
        inverse = jax.scipy.linalg.solve_triangular(diag_block, identity, lower=True)
        rows_cbar = grad_nat[:, col_start:col_end] - trail_part[:, col_start:col_end] - product(adj_rows, below_diag)
        cross_part = product(adj_rows.T, factor_nat[:, col_start:col_end])
        top_masked = jnp.where(row_index >= col_end, top_grad[:, col_start:col_end], 0.0)
        top_cbar = top_masked - (product(adj_top + adj_top.T, below_diag) + cross_part)
        rows_adj = product(rows_cbar, inverse)
        top_adj = product(top_cbar, inverse)
        diag_grad = jnp.tril(top_grad[col_start:col_end, col_start:col_end] - product(top_adj.T, below_diag) - product(rows_adj.T, factor_nat[:, col_start:col_end]))
        diag_adjoint = cholesky_adjoint(diag_block, inverse, diag_grad)
        adj_rows = adj_rows.at[:, col_start:col_end].set(rows_adj)
        adj_top = adj_top.at[:, col_start:col_end].set(top_adj.at[col_start:col_end].set(diag_adjoint))
    return (stored_order(adj_rows, N_ROW), adj_top)
```

```python
import functools

import jax
import jax.numpy as jnp
import numpy as np
from jax import lax
from jax.experimental import pallas as pl
from jax.experimental.pallas import tpu as pltpu
from jax.sharding import PartitionSpec as P

NB = 256
NP = 3
CB = 128
LEAF = 32

exact_dots = lax.Precision.HIGHEST
split_dots = lax.Precision.HIGH


def dims_dot(left, right, left_dim, right_dim, precision=exact_dots):
    return lax.dot_general(
        left,
        right,
        (((left_dim,), (right_dim,)), ((), ())),
        precision=precision,
        preferred_element_type=jnp.float32,
    )


def product(left, right):
    return dims_dot(left, right, 1, 0)


def lower_half(matrix):
    row_ids = lax.broadcasted_iota(jnp.int32, matrix.shape, 0)
    col_ids = lax.broadcasted_iota(jnp.int32, matrix.shape, 1)
    return jnp.where(row_ids > col_ids, matrix, jnp.where(row_ids == col_ids, 0.5 * matrix, 0.0))


def inverse_kernel(leaf_ref, factor_ref, out_ref, leaf_out):
    width = factor_ref.shape[0]
    dot = functools.partial(jnp.dot, precision=exact_dots, preferred_element_type=jnp.float32)
    lane = lax.broadcasted_iota(jnp.int32, (1, width), 1) % LEAF
    row_at = lax.broadcasted_iota(jnp.int32, (LEAF, width), 0)
    leaf_out[...] = jnp.zeros_like(leaf_out)
    for row in range(LEAF):
        known = leaf_ref[row]
        diag = known[row : row + 1]
        total = jnp.sum(jnp.where(row_at < row, known * leaf_out[...], 0.0), axis=0, keepdims=True)
        leaf_out[row : row + 1] = (jnp.where(lane == row, 1.0, 0.0) - total) / diag
    out_ref[...] = jnp.zeros_like(out_ref)
    for at in range(0, width, CB):
        spread = jnp.concatenate([leaf_out[:, at : at + CB]] * (CB // LEAF), 0)
        rows = lax.broadcasted_iota(jnp.int32, (CB, CB), 0)
        cols = lax.broadcasted_iota(jnp.int32, (CB, CB), 1)
        inv = jnp.where(rows // LEAF == cols // LEAF, spread, 0.0)
        block = factor_ref[at : at + CB, at : at + CB]
        size = LEAF
        while size < CB:
            below = (rows // size == cols // size + 1) & (rows // (2 * size) == cols // (2 * size))
            inv = inv - dot(dot(inv, jnp.where(below, block, 0.0)), inv)
            size *= 2
        out_ref[at : at + CB, at : at + CB] = inv
    for at in range(0, width, NB):
        size = CB
        while size < NB:
            for low in range(at, at + NB, 2 * size):
                mid, high = low + size, low + 2 * size
                first = out_ref[low:mid, low:mid]
                second = out_ref[mid:high, mid:high]
                out_ref[mid:high, low:mid] = -dot(dot(second, factor_ref[mid:high, low:mid]), first)
            size *= 2
    for at in range(NB, width, NB):
        carried = dot(factor_ref[at : at + NB, :at], out_ref[:at, :at])
        out_ref[at : at + NB, :at] = -dot(out_ref[at : at + NB, at : at + NB], carried)


def triangular_inverse(factor):
    width = factor.shape[0]
    leaves = width // LEAF
    blocks = jnp.stack(
        [factor[i * LEAF : (i + 1) * LEAF, i * LEAF : (i + 1) * LEAF] for i in range(leaves)], 2
    )
    spread = jnp.repeat(blocks, LEAF, axis=2)
    return pl.pallas_call(
        inverse_kernel,
        out_shape=jax.ShapeDtypeStruct((width, width), jnp.float32),
        in_specs=[pl.BlockSpec(memory_space=pltpu.VMEM)] * 2,
        out_specs=pl.BlockSpec(memory_space=pltpu.VMEM),
        scratch_shapes=[pltpu.VMEM((LEAF, width), jnp.float32)],
        compiler_params=pltpu.CompilerParams(vmem_limit_bytes=32 * 1024 * 1024),
        cost_estimate=pl.CostEstimate(flops=2 * width**3, bytes_accessed=16 * width**2, transcendentals=0),
    )(spread, factor)


def pick(blocks, which):
    return lax.dynamic_index_in_dim(blocks, which, 0, keepdims=False)


def swap(block, axis, offset):
    return lax.ppermute(block, axis, [(i, i ^ offset) for i in range(lax.axis_size(axis))])


def exchange(blocks, axis):
    here = lax.axis_index(axis)
    size = lax.axis_size(axis)
    arrived = [pick(blocks, here)]
    arrived += [swap(pick(blocks, here ^ offset), axis, offset) for offset in range(1, size)]
    stacked = jnp.stack(arrived)
    return [pick(stacked, here ^ i) for i in range(size)]


def align_rows(panel):
    col_owners, row_owners = lax.axis_size("col"), lax.axis_size("row")
    width, owned = panel.shape
    part = owned // col_owners
    pieces = panel.reshape(width, col_owners, part).transpose(1, 0, 2)
    from_cols = exchange(pieces, "col")
    per_row = col_owners // row_owners
    tile = min(CB, part)
    for_rows = []
    for row in range(row_owners):
        parts = [from_cols[each * row_owners + row] for each in range(per_row)]
        cuts = [
            cut[:, at : at + tile] for at in range(0, part, tile) for cut in parts
        ]
        for_rows.append(jnp.concatenate(cuts, 1))
    return jnp.concatenate(exchange(jnp.stack(for_rows), "row"), 0)


def gather_panels(panel):
    row_owners = lax.axis_size("row")
    half = panel.shape[0] // 2
    have = {0: (panel[:half], panel[half:])}
    for offset in range(1, row_owners):
        low = offset & -offset
        high = 1 << (offset.bit_length() - 1)
        have[offset] = (
            swap(have[offset ^ low][0], "row", low),
            swap(have[offset ^ high][1], "row", high),
        )
    return [jnp.concatenate(have[offset], 0) for offset in range(row_owners)]


def sum_over_cols(partial):
    planes = lax.axis_size("col") // 2
    width = partial.shape[0]
    here = lax.axis_index("col")
    plane, core = here // 2, here % 2
    blocks = partial.reshape(width, planes, 2, -1).transpose(2, 1, 0, 3)
    mine = pick(blocks, core) + swap(pick(blocks, 1 - core), "col", 1)
    rising = falling = None
    for hops in range(planes - 1, 0, -1):
        up = pick(mine, jnp.minimum(plane + hops, planes - 1))
        down = pick(mine, jnp.maximum(plane - hops, 0))
        if rising is not None:
            up, down = up + rising, down + falling
        pairs = [(2 * at + k, 2 * at + 2 + k) for at in range(planes - hops) for k in range(2)]
        rising = lax.ppermute(up, "col", pairs)
        falling = lax.ppermute(down, "col", [(2 * planes - 1 - a, 2 * planes - 1 - b) for a, b in pairs])
    return pick(mine, plane) + rising + falling


def sum_everywhere(block, least):
    order = [("col", 1)]
    order += [("row", 1 << b) for b in range(lax.axis_size("row").bit_length() - 1)]
    order += [("col", 1 << b) for b in range(1, lax.axis_size("col").bit_length() - 1)]
    halved = []
    for axis, bit in order:
        rows = block.shape[0]
        if rows // 2 >= least and rows % 16 == 0:
            upper = (lax.axis_index(axis) & bit) != 0
            low, high = block[: rows // 2], block[rows // 2 :]
            block = jnp.where(upper, high, low) + swap(jnp.where(upper, low, high), axis, bit)
            halved.append((axis, bit, upper))
        else:
            block = block + swap(block, axis, bit)
    for axis, bit, upper in reversed(halved):
        other = swap(block, axis, bit)
        block = jnp.concatenate([jnp.where(upper, other, block), jnp.where(upper, block, other)], 0)
    return block


def slot_table(row_owners):
    table = []
    for row in range(row_owners):
        rest = [row ^ (1 << b) for b in range(row_owners.bit_length() - 1)]
        second = max(rest)
        others = [c for c in range(row_owners - 1, -1, -1) if c not in (row, second)]
        table.append([row, second] + others)
    return np.array(table)


def per_device(trail_grad, factor_rows, factor_top, rows_grad, top_grad):
    row_owner = lax.axis_index("row")
    row_owners = lax.axis_size("row")
    panel_width = factor_top.shape[0]
    chunk = factor_rows.shape[1]
    own_panel = factor_rows.T
    table = slot_table(row_owners)
    late = len(set(table[:, -1]))
    split = late * chunk

    panels = gather_panels(own_panel)
    aligned = align_rows(own_panel)
    grad_chunks = rows_grad.T.reshape(row_owners, chunk, -1)
    inverse = triangular_inverse(factor_top)

    adjoint_rows = jnp.zeros_like(grad_chunks)
    inner = jnp.zeros((row_owners, chunk, panel_width), jnp.float32)
    for slot in range(row_owners):
        which = jnp.asarray(table[:, slot])[row_owner]
        offsets = sorted({int(table[r, slot]) ^ r for r in range(row_owners)})
        panel = panels[offsets[0]]
        for offset in offsets[1:]:
            panel = jnp.where((which ^ row_owner) == offset, panels[offset], panel)
        partial = dims_dot(panel, trail_grad, 1, 1, split_dots)
        rest = pick(grad_chunks, which) - 2.0 * sum_over_cols(partial)
        adjoint_rows = lax.dynamic_update_index_in_dim(adjoint_rows, rest, which, 0)
        inner = lax.dynamic_update_index_in_dim(inner, dims_dot(rest, aligned, 1, 1), which, 0)
        if slot == row_owners - 2:
            early = inner[late:].reshape(-1, panel_width)
    early = sum_everywhere(early, 8)
    last = sum_everywhere(inner[:late].reshape(split, panel_width)[:, :split], 64)

    adjoint_rows = adjoint_rows.reshape(panel_width, -1)
    rows_out = dims_dot(adjoint_rows, inverse, 0, 0, split_dots)

    lo, hi = slice(0, split), slice(split, panel_width)
    inv_lo, inv_hi, inv_mix = inverse[lo, lo], inverse[hi, hi], inverse[hi, lo]
    fac_lo, fac_hi, fac_mix = factor_top[lo, lo], factor_top[hi, hi], factor_top[hi, lo]
    moved = dims_dot(inv_hi, early, 0, 0)
    bar_mix = top_grad[hi, lo] - moved[:, lo]
    bar_hi = jnp.tril(top_grad[hi, hi] - moved[:, hi])
    mid_mix = dims_dot(fac_hi, bar_mix, 0, 0)
    mid_hi = lower_half(dims_dot(fac_hi, bar_hi, 0, 0))
    left_mix = dims_dot(inv_hi, mid_mix, 0, 0)
    left_hi = dims_dot(inv_hi, mid_hi, 0, 0)
    left_over = dims_dot(inv_mix, mid_hi, 0, 0)
    out_hi = product(left_hi, inv_hi)
    out_mix = product(left_mix, inv_lo) + product(left_hi, inv_mix) + product(left_over, inv_hi).T
    out_hi = lower_half(out_hi + out_hi.T)
    bar_known = top_grad[lo, lo] - dims_dot(inv_mix, early[:, lo], 0, 0)
    mid_known = dims_dot(fac_mix, bar_mix, 0, 0)
    left_known = dims_dot(inv_mix, mid_mix, 0, 0)
    out_known = product(left_over, inv_mix)

    bar_lo = jnp.tril(bar_known - dims_dot(inv_lo, last, 0, 0))
    mid_lo = lower_half(dims_dot(fac_lo, bar_lo, 0, 0) + mid_known)
    left_lo = dims_dot(inv_lo, mid_lo, 0, 0) + left_known
    out_lo = product(left_lo, inv_lo) + out_known
    out_lo = lower_half(out_lo + out_lo.T)
    top_out = jnp.concatenate(
        [
            jnp.concatenate([out_lo, jnp.zeros_like(out_mix.T)], 1),
            jnp.concatenate([out_mix, out_hi], 1),
        ],
        0,
    )
    return rows_out, top_out


def solution(mesh):
    placed = (P("row", "col"), P("col", "row"), P(), P(("row", "col"), None), P())
    return jax.shard_map(
        per_device,
        mesh=mesh,
        in_specs=placed,
        out_specs=(P(("row", "col"), None), P()),
        check_vma=False,
    )
```

```python
import functools

import jax
import jax.numpy as jnp
import numpy as np
from jax import lax
from jax.experimental import pallas as pl
from jax.experimental.pallas import tpu as pltpu
from jax.sharding import PartitionSpec as P

NB = 256
NP = 3
CB = 128
LEAF = 32
VMEM_LIMIT = 48 * 1024 * 1024
WEIGHTS = (4.0, 2.0, 2.0)

exact_dots = lax.Precision.HIGHEST
split_dots = lax.Precision.HIGH


def dims_dot(left, right, left_dim, right_dim, precision=exact_dots):
    return lax.dot_general(
        left,
        right,
        (((left_dim,), (right_dim,)), ((), ())),
        precision=precision,
        preferred_element_type=jnp.float32,
    )


def product(left, right):
    return dims_dot(left, right, 1, 0)


def lower_half(matrix):
    row_ids = lax.broadcasted_iota(jnp.int32, matrix.shape, 0)
    col_ids = lax.broadcasted_iota(jnp.int32, matrix.shape, 1)
    return jnp.where(row_ids > col_ids, matrix, jnp.where(row_ids == col_ids, 0.5 * matrix, 0.0))


def inverse_kernel(factor_ref, out_ref, spread_ref, leaf_out):
    width = factor_ref.shape[0]
    dot = functools.partial(jnp.dot, precision=exact_dots, preferred_element_type=jnp.float32)
    rows = lax.broadcasted_iota(jnp.int32, (CB, CB), 0)
    cols = lax.broadcasted_iota(jnp.int32, (CB, CB), 1)
    same_leaf = rows // LEAF == cols // LEAF
    ones = jnp.where(same_leaf, 1.0, 0.0)
    lane_at = lax.broadcasted_iota(jnp.int32, (LEAF, CB), 1) % LEAF
    for at in range(0, width, CB):
        turned = jnp.where(same_leaf, factor_ref[at : at + CB, at : at + CB], 0.0).T
        leaves = sum(turned[low : low + LEAF] for low in range(0, CB, LEAF))
        picked = jnp.concatenate(
            [jnp.where(lane_at == row, leaves, 0.0) for row in range(LEAF)], 0
        )
        spread_ref[:, at : at + CB] = dot(picked, ones)
    lane = lax.broadcasted_iota(jnp.int32, (1, width), 1) % LEAF
    row_at = lax.broadcasted_iota(jnp.int32, (LEAF, width), 0)
    leaf_out[...] = jnp.zeros_like(leaf_out)
    for row in range(LEAF):
        known = spread_ref[row * LEAF : (row + 1) * LEAF]
        diag = known[row : row + 1]
        total = jnp.sum(jnp.where(row_at < row, known * leaf_out[...], 0.0), axis=0, keepdims=True)
        leaf_out[row : row + 1] = (jnp.where(lane == row, 1.0, 0.0) - total) / diag
    out_ref[...] = jnp.zeros_like(out_ref)
    for at in range(0, width, CB):
        spread = jnp.concatenate([leaf_out[:, at : at + CB]] * (CB // LEAF), 0)
        inv = jnp.where(same_leaf, spread, 0.0)
        block = factor_ref[at : at + CB, at : at + CB]
        size = LEAF
        while size < CB:
            below = (rows // size == cols // size + 1) & (rows // (2 * size) == cols // (2 * size))
            inv = inv - dot(dot(inv, jnp.where(below, block, 0.0)), inv)
            size *= 2
        out_ref[at : at + CB, at : at + CB] = inv
    for at in range(0, width, NB):
        size = CB
        while size < NB:
            for low in range(at, at + NB, 2 * size):
                mid, high = low + size, low + 2 * size
                first = out_ref[low:mid, low:mid]
                second = out_ref[mid:high, mid:high]
                out_ref[mid:high, low:mid] = -dot(dot(second, factor_ref[mid:high, low:mid]), first)
            size *= 2
    for at in range(NB, width, NB):
        carried = dot(factor_ref[at : at + NB, :at], out_ref[:at, :at])
        out_ref[at : at + NB, :at] = -dot(out_ref[at : at + NB, at : at + NB], carried)


def cost(flops):
    return pl.CostEstimate(flops=int(flops), bytes_accessed=1024, transcendentals=0)


def whole_in_vmem(kernel, out_shape, scratch, operands, flops, scalars=None, after=()):
    first = () if scalars is None else (scalars,)

    def body(*refs):
        head = refs[: len(first)]
        inputs = refs[len(first) : len(first) + len(operands)]
        rest = refs[len(first) + len(operands) + len(after) :]
        kernel(*head, *inputs, *rest)

    return pl.pallas_call(
        body,
        out_shape=out_shape,
        in_specs=[pl.BlockSpec(memory_space=pltpu.SMEM)] * len(first)
        + [pl.BlockSpec(memory_space=pltpu.VMEM)] * len(operands)
        + [pl.BlockSpec(memory_space=pl.ANY)] * len(after),
        out_specs=jax.tree.map(lambda _: pl.BlockSpec(memory_space=pltpu.VMEM), out_shape),
        scratch_shapes=scratch,
        compiler_params=pltpu.CompilerParams(vmem_limit_bytes=VMEM_LIMIT),
        cost_estimate=cost(flops),
    )(*first, *operands, *after)


def triangular_inverse(factor, after):
    width = factor.shape[0]
    return whole_in_vmem(
        inverse_kernel,
        jax.ShapeDtypeStruct((width, width), jnp.float32),
        [pltpu.VMEM((LEAF * LEAF, width), jnp.float32), pltpu.VMEM((LEAF, width), jnp.float32)],
        [factor],
        1024,
        after=after,
    )


def turned_product(left, right):
    return product(left.T, right)


def early_kernel(inner, inv_hi, inv_lo, fac_hi, fac_mix, top_hi, top_mix, top_lo, out_hi, out_mix, base):
    split = inv_lo.shape[0]
    turned = inv_hi[...].T
    moved = product(turned, inner[...])
    lower = jnp.tril(top_hi[...] - moved[:, split:])
    middle = lower_half(turned_product(fac_hi[...], lower))
    whole = product(product(turned, middle), inv_hi[...])
    whole = whole + whole.T
    out_hi[...] = lower_half(whole)
    moved = moved[:, :split]
    mixed = product(top_mix[...] - moved - product(whole, fac_mix[...]), inv_lo[...])
    out_mix[...] = mixed
    known = turned_product(inv_lo[...], turned_product(fac_mix[...], moved))
    base[...] = top_lo[...] + known - turned_product(mixed, fac_mix[...])


def last_kernel(inner, inv, fac, base, result):
    turned = inv[...].T
    lower = jnp.tril(base[...] - product(turned, inner[...]))
    middle = lower_half(turned_product(fac[...], lower))
    whole = product(product(turned, middle), inv[...])
    result[...] = lower_half(whole + whole.T)


def pack_kernel(at_ref, first_ref, second_ref, stay_ref, go_ref):
    stay_ref[0] = first_ref[...]
    go_ref[0] = second_ref[...]


def pack_panel(panel, after=()):
    width, owned = panel.shape
    owners = lax.axis_size("col")
    part = owned // owners
    here = lax.axis_index("col")
    if part % CB:
        blocks = panel.reshape(width, owners, part).transpose(1, 0, 2)
        blocks = jnp.take(blocks, jnp.arange(owners) ^ here, axis=0)
        return blocks[0::2], blocks[1::2]
    shape = jax.ShapeDtypeStruct((owners // 2, width, part), jnp.float32)
    out_spec = pl.BlockSpec((1, width, part), lambda j, at: (j, 0, 0))
    return pl.pallas_call(
        pack_kernel,
        out_shape=(shape, shape),
        grid_spec=pltpu.PrefetchScalarGridSpec(
            num_scalar_prefetch=1,
            grid=(owners // 2,),
            in_specs=[
                pl.BlockSpec((width, part), lambda j, at: (0, (2 * j) ^ at[0])),
                pl.BlockSpec((width, part), lambda j, at: (0, (2 * j + 1) ^ at[0])),
            ],
            out_specs=(out_spec, out_spec),
        ),
        compiler_params=pltpu.CompilerParams(vmem_limit_bytes=VMEM_LIMIT),
        cost_estimate=cost(8 * 256 * panel.size),
    )(jnp.full((1,), here, jnp.int32), panel, panel)


def regroup_kernel(tile, at_ref, *refs):
    pairs, out_ref, blocks_ref = refs[:-2], refs[-2], refs[-1]
    owners, _, part = blocks_ref.shape
    rows = out_ref.shape[0]
    for j, pair in enumerate(pairs):
        blocks_ref[2 * j] = pair[0]
        blocks_ref[2 * j + 1] = pair[1]
    for offset in range(rows):
        lane = 0
        for q in range(0, part, tile):
            for group in range(owners // rows):
                source = (at_ref[0] ^ offset) + rows * (group ^ at_ref[1])
                out_ref[offset, :, lane : lane + tile] = blocks_ref[source, :, q : q + tile]
                lane += tile


def place_kernel(at_ref, *refs):
    pieces, out_ref = refs[:-1], refs[-1]
    for offset, piece in enumerate(pieces):
        out_ref[at_ref[0] ^ offset] = piece[...]


def align_rows(pairs, after):
    width, part = pairs[0].shape[1:]
    owners = 2 * len(pairs)
    row_owners = lax.axis_size("row")
    here = lax.axis_index("col")
    row = lax.axis_index("row")
    rows = part * owners // row_owners
    at = jnp.stack([(here % row_owners) ^ row, here // row_owners]).astype(jnp.int32)
    grouped = whole_in_vmem(
        functools.partial(regroup_kernel, min(CB, part)),
        jax.ShapeDtypeStruct((row_owners, width, rows), jnp.float32),
        [pltpu.VMEM((owners, width, part), jnp.float32)],
        pairs,
        4 * 256 * owners * width * part,
        scalars=at,
        after=after,
    )
    arrived = [grouped[0]]
    arrived += [swap(grouped[offset], "row", offset) for offset in range(1, row_owners)]
    aligned = whole_in_vmem(
        place_kernel,
        jax.ShapeDtypeStruct((row_owners, width, rows), jnp.float32),
        [],
        arrived,
        4 * 256 * owners * width * part,
        scalars=jnp.full((1,), row, jnp.int32),
    )
    return aligned.reshape(row_owners * width, rows), grouped


def settle_kernel(at_ref, summed, grads, aligned, rest_out, inner_out):
    rest = grads[at_ref[0]] - 2.0 * summed[...]
    rest_out[...] = rest
    inner_out[...] = dims_dot(rest, aligned[...], 1, 1)


def adjoint_kernel(at_ref, inverse, *refs):
    total = 0.0
    for slot, rest in enumerate(refs[:-1]):
        total += turned_product(rest[...], inverse[at_ref[slot]])
    refs[-1][...] = total


def neighbour_panels(panel):
    bits = lax.axis_size("row").bit_length() - 1
    return {0: [panel]} | {1 << b: [swap(panel, "row", 1 << b)] for b in range(bits)}


def copy_kernel(source, target):
    target[...] = source[...]


def stage_kernel(panel, stay, arrived, later, *pairs):
    later[...] = panel[...]
    for j, pair in enumerate(pairs):
        pair[0] = stay[j]
        pair[1] = arrived[j]


def stage(panel, stay, arrived, after):
    shapes = [jax.ShapeDtypeStruct(panel.shape, jnp.float32)]
    shapes += [jax.ShapeDtypeStruct((2,) + stay.shape[1:], jnp.float32)] * stay.shape[0]
    later, *pairs = whole_in_vmem(
        stage_kernel, shapes, [], [panel, stay, arrived], 8 * 256 * panel.size, after=after
    )
    return later, pairs


def times_trail_kernel(offsets, counts, at_ref, *refs):
    panel_refs, trail_ref = refs[: sum(counts)], refs[sum(counts)]
    out_ref, panel_at, high_at, low_at = refs[-4:]

    @pl.when(pl.program_id(0) == 0)
    def _():
        first = 0
        for offset, count in zip(offsets, counts):
            pieces = panel_refs[first : first + count]
            first += count

            @pl.when(at_ref[0] == offset)
            def _():
                row = 0
                for piece in pieces:
                    panel_at[row : row + piece.shape[0]] = piece[...]
                    row += piece.shape[0]

        panel = panel_at[...]
        high = panel.astype(jnp.bfloat16)
        high_at[...] = high
        low_at[...] = (panel - high.astype(jnp.float32)).astype(jnp.bfloat16)

    depth = trail_ref.shape[1]
    step = min(depth, 2 * NB)
    total = jnp.zeros(out_ref.shape[1:], jnp.float32)
    for k in range(0, depth, step):
        trail = trail_ref[:, k : k + step]
        high = trail.astype(jnp.bfloat16)
        low = (trail - high.astype(jnp.float32)).astype(jnp.bfloat16)
        for left, right in (
            (low_at[:, k : k + step], high),
            (high_at[:, k : k + step], low),
            (high_at[:, k : k + step], high),
        ):
            total += dims_dot(left, right, 1, 1, None)
    out_ref[0] = total


def times_trail(candidates, offset, core, trail, weight, after=()):
    offsets = tuple(candidates)
    counts = tuple(len(candidates[each]) for each in offsets)
    pieces = [piece for each in offsets for piece in candidates[each]]
    width = sum(piece.shape[0] for piece in candidates[offsets[0]])
    depth = trail.shape[1]
    planes = lax.axis_size("col") // 2
    rows = trail.shape[0] // (2 * planes)
    at = jnp.stack([offset, core]).astype(jnp.int32)
    return pl.pallas_call(
        functools.partial(times_trail_kernel, offsets, counts),
        out_shape=jax.ShapeDtypeStruct((planes, width, rows), jnp.float32),
        grid_spec=pltpu.PrefetchScalarGridSpec(
            num_scalar_prefetch=1,
            grid=(planes,),
            in_specs=[pl.BlockSpec(piece.shape, lambda j, at: (0, 0)) for piece in pieces]
            + [pl.BlockSpec((rows, depth), lambda j, at: (2 * j + at[1], 0))]
            + [pl.BlockSpec(memory_space=pl.ANY)] * len(after),
            out_specs=pl.BlockSpec((1, width, rows), lambda j, at: (j, 0, 0)),
            scratch_shapes=[
                pltpu.VMEM((width, depth), jnp.float32),
                pltpu.VMEM((width, depth), jnp.bfloat16),
                pltpu.VMEM((width, depth), jnp.bfloat16),
            ],
        ),
        compiler_params=pltpu.CompilerParams(vmem_limit_bytes=VMEM_LIMIT),
        cost_estimate=cost(weight * 8.6 * width * depth * rows * planes),
    )(at, *pieces, trail, *after)


def sum_over_planes(block):
    planes, width, rows = block.shape
    groups = [[2 * plane + core for plane in range(planes)] for core in range(2)]
    return lax.psum_scatter(
        block.reshape(planes * width, rows),
        "col",
        scatter_dimension=0,
        tiled=True,
        axis_index_groups=groups,
    )


def pick(blocks, which):
    return lax.dynamic_index_in_dim(blocks, which, 0, keepdims=False)


def swap(block, axis, offset):
    return lax.ppermute(block, axis, [(i, i ^ offset) for i in range(lax.axis_size(axis))])


def sum_shares(block, least):
    order = [("col", 1)]
    order += [("row", 1 << b) for b in range(lax.axis_size("row").bit_length() - 1)]
    order += [("col", 1 << b) for b in range(1, lax.axis_size("col").bit_length() - 1)]
    halved = []
    for axis, bit in order:
        rows = block.shape[0]
        if rows // 2 >= least and rows % 16 == 0:
            upper = (lax.axis_index(axis) & bit) != 0
            low, high = block[: rows // 2], block[rows // 2 :]
            block = jnp.where(upper, high, low) + swap(jnp.where(upper, low, high), axis, bit)
            halved.append((axis, bit, upper))
        else:
            block = block + swap(block, axis, bit)
    return block, halved


def join_shares(block, halved):
    for axis, bit, upper in reversed(halved):
        other = swap(block, axis, bit)
        block = jnp.concatenate([jnp.where(upper, other, block), jnp.where(upper, block, other)], 0)
    return block


def slot_table(row_owners):
    table = []
    for row in range(row_owners):
        rest = [row ^ (1 << b) for b in range(row_owners.bit_length() - 1)]
        second = max(rest)
        others = [c for c in range(row_owners - 1, -1, -1) if c not in (row, second)]
        table.append([row, second] + others)
    return np.array(table)


def per_device(trail_grad, factor_rows, factor_top, rows_grad, top_grad):
    row_owner = lax.axis_index("row")
    row_owners = lax.axis_size("row")
    core = lax.axis_index("col") % 2
    panel_width = factor_top.shape[0]
    chunk = factor_rows.shape[1]
    own_rows = rows_grad.shape[0]
    table = slot_table(row_owners)
    late = len(set(table[:, -1]))
    split = late * chunk
    whiches = [jnp.asarray(table[:, slot])[row_owner] for slot in range(row_owners)]

    own_panel = factor_rows.T
    stay, go = pack_panel(own_panel)
    arrived = swap(go, "col", 1)
    panels = neighbour_panels(own_panel)

    def multiply(slot, after):
        offset = whiches[slot] ^ row_owner
        offsets = sorted({int(table[r, slot]) ^ r for r in range(row_owners)})
        candidates = {each: panels[each] for each in offsets}
        theirs = times_trail(candidates, offset, 1 - core, trail_grad, WEIGHTS[min(slot, 2)], after)
        ours = times_trail(candidates, offset, core, trail_grad, WEIGHTS[min(slot, 2)], (theirs,))
        total = ours + swap(theirs, "col", 1)
        return sum_over_planes(total), total

    def settle(slot, after=()):
        shapes = [
            jax.ShapeDtypeStruct((chunk, own_rows), jnp.float32),
            jax.ShapeDtypeStruct((chunk, panel_width), jnp.float32),
        ]
        return whole_in_vmem(
            settle_kernel,
            shapes,
            [],
            [waiting[slot], grads, aligned],
            1024,
            scalars=jnp.full((1,), whiches[slot], jnp.int32),
            after=after,
        )

    grads = rows_grad.T.reshape(row_owners, chunk, own_rows)
    planes = stay.shape[0]
    first = planes // 2
    ahead = swap(jnp.stack([stay[first], arrived[first]]), "col", 2 * first)
    summed, done = multiply(0, (arrived,))
    waiting = [summed]
    later, pairs = stage(own_panel, stay, arrived, (done, ahead))
    for offset in range(1, row_owners):
        if offset not in panels:
            panels[offset] = [swap(later, "row", offset)]
    pairs = [
        pairs[0] if j == 0 else ahead if j == first else swap(pairs[j], "col", 2 * j)
        for j in range(planes)
    ]
    done = later
    for slot in range(1, row_owners):
        if slot == 2:
            inverse = done = triangular_inverse(factor_top, (done,))
        if slot == row_owners - 1:
            aligned, done = align_rows(pairs, (done,))
        before = (waiting[slot - 2],) if slot >= 2 else ()
        summed, done = multiply(slot, (done, *before))
        waiting.append(summed)
    rests, inner = [], []
    for slot in range(row_owners - 1):
        rest, part = settle(slot, (done,))
        rests.append(rest)
        inner.append(part)
    early = jnp.concatenate(
        [
            sum(jnp.where(whiches[s] == each, inner[s], 0.0) for s in range(row_owners - 1))
            for each in range(late, row_owners)
        ],
        0,
    )
    share, halved = sum_shares(early, 8)
    rest, part = settle(row_owners - 1)
    rests.append(rest)
    share = whole_in_vmem(
        copy_kernel,
        jax.ShapeDtypeStruct(share.shape, jnp.float32),
        [],
        [share],
        1024,
        after=(part,),
    )
    early = join_shares(share, halved)
    inner.append(part)
    adjoint = whole_in_vmem(
        adjoint_kernel,
        jax.ShapeDtypeStruct((own_rows, panel_width), jnp.float32),
        [],
        [inverse.reshape(row_owners, chunk, panel_width), *rests],
        24 * own_rows * panel_width**2,
        scalars=jnp.stack(whiches).astype(jnp.int32),
    )
    last = jnp.concatenate(
        [
            sum(jnp.where(whiches[s] == each, inner[s][:, :split], 0.0) for s in range(row_owners))
            for each in range(late)
        ],
        0,
    )
    last = join_shares(*sum_shares(last, 64))

    lo, hi = slice(0, split), slice(split, panel_width)
    rest = panel_width - split
    out_hi, out_mix, base = whole_in_vmem(
        early_kernel,
        [jax.ShapeDtypeStruct(each, jnp.float32) for each in ((rest, rest), (rest, split), (split, split))],
        [],
        [
            early,
            inverse[hi, hi],
            inverse[lo, lo],
            factor_top[hi, hi],
            factor_top[hi, lo],
            top_grad[hi, hi],
            top_grad[hi, lo],
            top_grad[lo, lo],
        ],
        36 * panel_width**3,
    )
    out_lo = whole_in_vmem(
        last_kernel,
        jax.ShapeDtypeStruct((split, split), jnp.float32),
        [],
        [last, inverse[lo, lo], factor_top[lo, lo], base],
        14 * panel_width**3,
    )
    top_out = jnp.concatenate(
        [
            jnp.concatenate([out_lo, jnp.zeros((split, rest), jnp.float32)], 1),
            jnp.concatenate([out_mix, out_hi], 1),
        ],
        0,
    )
    return adjoint, top_out


def solution(mesh):
    placed = (P("row", "col"), P("col", "row"), P(), P(("row", "col"), None), P())
    return jax.shard_map(
        per_device,
        mesh=mesh,
        in_specs=placed,
        out_specs=(P(("row", "col"), None), P()),
        check_vma=False,
    )
```

```python
import functools

import jax
import jax.numpy as jnp
import numpy as np
from jax import lax
from jax.experimental import pallas as pl
from jax.experimental.pallas import tpu as pltpu
from jax.sharding import PartitionSpec as P

NB = 256
NP = 3
CB = 128
LEAF = 32
STEPS = 4
VMEM_LIMIT = 48 * 1024 * 1024
WEIGHTS = (4.0, 0.4, 2.0)

exact_dots = lax.Precision.HIGHEST
split_dots = lax.Precision.HIGH


def dims_dot(left, right, left_dim, right_dim, precision=exact_dots):
    return lax.dot_general(
        left,
        right,
        (((left_dim,), (right_dim,)), ((), ())),
        precision=precision,
        preferred_element_type=jnp.float32,
    )


def product(left, right):
    return dims_dot(left, right, 1, 0)


def lower_half(matrix):
    row_ids = lax.broadcasted_iota(jnp.int32, matrix.shape, 0)
    col_ids = lax.broadcasted_iota(jnp.int32, matrix.shape, 1)
    return jnp.where(row_ids > col_ids, matrix, jnp.where(row_ids == col_ids, 0.5 * matrix, 0.0))


def inverse_kernel(factor_ref, out_ref, spread_ref, leaf_out):
    width = factor_ref.shape[0]
    dot = functools.partial(jnp.dot, precision=exact_dots, preferred_element_type=jnp.float32)
    rows = lax.broadcasted_iota(jnp.int32, (CB, CB), 0)
    cols = lax.broadcasted_iota(jnp.int32, (CB, CB), 1)
    same_leaf = rows // LEAF == cols // LEAF
    ones = jnp.where(same_leaf, 1.0, 0.0)
    lane_at = lax.broadcasted_iota(jnp.int32, (LEAF, CB), 1) % LEAF
    for at in range(0, width, CB):
        turned = jnp.where(same_leaf, factor_ref[at : at + CB, at : at + CB], 0.0).T
        leaves = sum(turned[low : low + LEAF] for low in range(0, CB, LEAF))
        picked = jnp.concatenate(
            [jnp.where(lane_at == row, leaves, 0.0) for row in range(LEAF)], 0
        )
        spread_ref[:, at : at + CB] = dot(picked, ones)
    lane = lax.broadcasted_iota(jnp.int32, (1, width), 1) % LEAF
    row_at = lax.broadcasted_iota(jnp.int32, (LEAF, width), 0)
    leaf_out[...] = jnp.zeros_like(leaf_out)
    for row in range(LEAF):
        known = spread_ref[row * LEAF : (row + 1) * LEAF]
        diag = known[row : row + 1]
        total = jnp.sum(jnp.where(row_at < row, known * leaf_out[...], 0.0), axis=0, keepdims=True)
        leaf_out[row : row + 1] = (jnp.where(lane == row, 1.0, 0.0) - total) / diag
    out_ref[...] = jnp.zeros_like(out_ref)
    for at in range(0, width, CB):
        spread = jnp.concatenate([leaf_out[:, at : at + CB]] * (CB // LEAF), 0)
        inv = jnp.where(same_leaf, spread, 0.0)
        block = factor_ref[at : at + CB, at : at + CB]
        size = LEAF
        while size < CB:
            below = (rows // size == cols // size + 1) & (rows // (2 * size) == cols // (2 * size))
            inv = inv - dot(dot(inv, jnp.where(below, block, 0.0)), inv)
            size *= 2
        out_ref[at : at + CB, at : at + CB] = inv
    for at in range(0, width, NB):
        size = CB
        while size < NB:
            for low in range(at, at + NB, 2 * size):
                mid, high = low + size, low + 2 * size
                first = out_ref[low:mid, low:mid]
                second = out_ref[mid:high, mid:high]
                out_ref[mid:high, low:mid] = -dot(dot(second, factor_ref[mid:high, low:mid]), first)
            size *= 2
    for at in range(NB, width, NB):
        carried = dot(factor_ref[at : at + NB, :at], out_ref[:at, :at])
        out_ref[at : at + NB, :at] = -dot(out_ref[at : at + NB, at : at + NB], carried)


def cost(flops):
    return pl.CostEstimate(flops=int(flops), bytes_accessed=1024, transcendentals=0)


def whole_in_vmem(kernel, out_shape, scratch, operands, flops, scalars=None, after=()):
    first = () if scalars is None else (scalars,)

    def body(*refs):
        head = refs[: len(first)]
        inputs = refs[len(first) : len(first) + len(operands)]
        rest = refs[len(first) + len(operands) + len(after) :]
        kernel(*head, *inputs, *rest)

    return pl.pallas_call(
        body,
        out_shape=out_shape,
        in_specs=[pl.BlockSpec(memory_space=pltpu.SMEM)] * len(first)
        + [pl.BlockSpec(memory_space=pltpu.VMEM)] * len(operands)
        + [pl.BlockSpec(memory_space=pl.ANY)] * len(after),
        out_specs=jax.tree.map(lambda _: pl.BlockSpec(memory_space=pltpu.VMEM), out_shape),
        scratch_shapes=scratch,
        compiler_params=pltpu.CompilerParams(vmem_limit_bytes=VMEM_LIMIT),
        cost_estimate=cost(flops),
    )(*first, *operands, *after)


def triangular_inverse(factor, after):
    width = factor.shape[0]
    return whole_in_vmem(
        inverse_kernel,
        jax.ShapeDtypeStruct((width, width), jnp.float32),
        [pltpu.VMEM((LEAF * LEAF, width), jnp.float32), pltpu.VMEM((LEAF, width), jnp.float32)],
        [factor],
        1024,
        after=after,
    )


def halves(matrix):
    high = matrix.astype(jnp.bfloat16)
    return high, (matrix - high.astype(jnp.float32)).astype(jnp.bfloat16)


def split_product(left, right):
    left_high, left_low = halves(left)
    right_high, right_low = halves(right)
    small = dims_dot(left_low, right_high, 1, 0, None) + dims_dot(left_high, right_low, 1, 0, None)
    return dims_dot(left_high, right_high, 1, 0, None) + small


def turned_split(left, right):
    return split_product(left.T, right)


def turned_product(left, right):
    return product(left.T, right)


def early_kernel(inner, inv_hi, inv_lo, fac_hi, fac_mix, top_hi, top_mix, top_lo, out_hi, out_mix, base):
    split = inv_lo.shape[0]
    turned = inv_hi[...].T
    moved = split_product(turned, inner[...])
    lower = jnp.tril(top_hi[...] - moved[:, split:])
    middle = lower_half(turned_split(fac_hi[...], lower))
    whole = split_product(split_product(turned, middle), inv_hi[...])
    whole = whole + whole.T
    out_hi[...] = lower_half(whole)
    moved = moved[:, :split]
    mixed = split_product(top_mix[...] - moved - split_product(whole, fac_mix[...]), inv_lo[...])
    out_mix[...] = mixed
    known = turned_split(inv_lo[...], turned_split(fac_mix[...], moved))
    base[...] = top_lo[...] + known - turned_split(mixed, fac_mix[...])


def last_kernel(inner, inv, fac, base, result):
    turned = inv[...].T
    lower = jnp.tril(base[...] - split_product(turned, inner[...]))
    middle = lower_half(turned_split(fac[...], lower))
    whole = split_product(split_product(turned, middle), inv[...])
    result[...] = lower_half(whole + whole.T)


def pack_kernel(at_ref, first_ref, second_ref, stay_ref, go_ref):
    stay_ref[0] = first_ref[...]
    go_ref[0] = second_ref[...]


def pack_panel(panel, after=()):
    width, owned = panel.shape
    owners = lax.axis_size("col")
    part = owned // owners
    here = lax.axis_index("col")
    if part % CB:
        blocks = panel.reshape(width, owners, part).transpose(1, 0, 2)
        blocks = jnp.take(blocks, jnp.arange(owners) ^ here, axis=0)
        return blocks[0::2], blocks[1::2]
    shape = jax.ShapeDtypeStruct((owners // 2, width, part), jnp.float32)
    out_spec = pl.BlockSpec((1, width, part), lambda j, at: (j, 0, 0))
    return pl.pallas_call(
        pack_kernel,
        out_shape=(shape, shape),
        grid_spec=pltpu.PrefetchScalarGridSpec(
            num_scalar_prefetch=1,
            grid=(owners // 2,),
            in_specs=[
                pl.BlockSpec((width, part), lambda j, at: (0, (2 * j) ^ at[0])),
                pl.BlockSpec((width, part), lambda j, at: (0, (2 * j + 1) ^ at[0])),
            ],
            out_specs=(out_spec, out_spec),
        ),
        compiler_params=pltpu.CompilerParams(vmem_limit_bytes=VMEM_LIMIT),
        cost_estimate=cost(8 * 256 * panel.size),
    )(jnp.full((1,), here, jnp.int32), panel, panel)


def regroup_kernel(tile, at_ref, *refs):
    pairs, out_ref, blocks_ref = refs[:-2], refs[-2], refs[-1]
    owners, _, part = blocks_ref.shape
    rows = out_ref.shape[0]
    for j, pair in enumerate(pairs):
        blocks_ref[2 * j] = pair[0]
        blocks_ref[2 * j + 1] = pair[1]
    for offset in range(rows):
        lane = 0
        for q in range(0, part, tile):
            for group in range(owners // rows):
                source = (at_ref[0] ^ offset) + rows * (group ^ at_ref[1])
                out_ref[offset, :, lane : lane + tile] = blocks_ref[source, :, q : q + tile]
                lane += tile


def place_kernel(at_ref, *refs):
    pieces, out_ref = refs[:-1], refs[-1]
    for offset, piece in enumerate(pieces):
        out_ref[at_ref[0] ^ offset] = piece[...]


def align_rows(pairs, after):
    width, part = pairs[0].shape[1:]
    owners = 2 * len(pairs)
    row_owners = lax.axis_size("row")
    here = lax.axis_index("col")
    row = lax.axis_index("row")
    rows = part * owners // row_owners
    at = jnp.stack([(here % row_owners) ^ row, here // row_owners]).astype(jnp.int32)
    grouped = whole_in_vmem(
        functools.partial(regroup_kernel, min(CB, part)),
        jax.ShapeDtypeStruct((row_owners, width, rows), jnp.float32),
        [pltpu.VMEM((owners, width, part), jnp.float32)],
        pairs,
        4 * 256 * owners * width * part,
        scalars=at,
        after=after,
    )
    arrived = [grouped[0]]
    arrived += [swap(grouped[offset], "row", offset) for offset in range(1, row_owners)]
    return arrived, grouped


def place_rows(arrived, after):
    row_owners = len(arrived)
    width, rows = arrived[0].shape
    aligned = whole_in_vmem(
        place_kernel,
        jax.ShapeDtypeStruct((row_owners, width, rows), jnp.float32),
        [],
        arrived,
        1024,
        scalars=jnp.full((1,), lax.axis_index("row"), jnp.int32),
        after=after,
    )
    return aligned.reshape(row_owners * width, rows)


def turn_kernel(source, target):
    turned = source[...].T
    chunk = target.shape[1]
    for at in range(target.shape[0]):
        target[at] = turned[at * chunk : (at + 1) * chunk]


def settle_kernel(at_ref, summed, grads, aligned, rest_out, inner_out):
    rest = grads[at_ref[0]] - 2.0 * summed[...]
    rest_out[...] = rest
    inner_out[...] = dims_dot(rest, aligned[...], 1, 1)


def adjoint_kernel(at_ref, inverse, *refs):
    count = at_ref.shape[0]
    rests, known, target = refs[:count], refs[count:-1], refs[-1]
    total = sum(each[...] for each in known)
    for slot, rest in enumerate(rests):
        total += turned_product(rest[...], inverse[at_ref[slot]])
    target[...] = total


def neighbour_panels(panel):
    bits = lax.axis_size("row").bit_length() - 1
    return {0: [panel]} | {1 << b: [swap(panel, "row", 1 << b)] for b in range(bits)}


def copy_kernel(source, target):
    target[...] = source[...]


def stage_kernel(panel, stay, arrived, later, *pairs):
    later[...] = panel[...]
    for j, pair in enumerate(pairs):
        pair[0] = stay[j]
        pair[1] = arrived[j]


def stage(panel, stay, arrived, after):
    shapes = [jax.ShapeDtypeStruct(panel.shape, jnp.float32)]
    shapes += [jax.ShapeDtypeStruct((2,) + stay.shape[1:], jnp.float32)] * stay.shape[0]
    later, *pairs = whole_in_vmem(
        stage_kernel, shapes, [], [panel, stay, arrived], 8 * 256 * panel.size, after=after
    )
    return later, pairs


def times_trail_kernel(offsets, counts, at_ref, *refs):
    panel_refs, trail_ref = refs[: sum(counts)], refs[sum(counts)]
    out_ref, panel_at, halves_at = refs[-3:]

    @pl.when(pl.program_id(0) == 0)
    def _():
        first = 0
        for offset, count in zip(offsets, counts):
            pieces = panel_refs[first : first + count]
            first += count

            @pl.when(at_ref[0] == offset)
            def _():
                row = 0
                for piece in pieces:
                    panel_at[row : row + piece.shape[0]] = piece[...]
                    row += piece.shape[0]

        panel = panel_at[...]
        high = panel.astype(jnp.bfloat16)
        halves_at[: panel.shape[0]] = high
        halves_at[panel.shape[0] :] = (panel - high.astype(jnp.float32)).astype(jnp.bfloat16)

    width = panel_at.shape[0]
    depth = trail_ref.shape[1]
    step = min(depth, 2 * NB)
    total = jnp.zeros(out_ref.shape[1:], jnp.float32)
    for k in range(0, depth, step):
        trail = trail_ref[:, k : k + step]
        high = trail.astype(jnp.bfloat16)
        low = (trail - high.astype(jnp.float32)).astype(jnp.bfloat16)
        both = dims_dot(halves_at[:, k : k + step], high, 1, 1, None)
        total += both[:width] + both[width:]
        total += dims_dot(halves_at[:width, k : k + step], low, 1, 1, None)
    out_ref[0] = total


def times_trail(candidates, offset, core, trail, weight, after=()):
    offsets = tuple(candidates)
    counts = tuple(len(candidates[each]) for each in offsets)
    pieces = [piece for each in offsets for piece in candidates[each]]
    width = sum(piece.shape[0] for piece in candidates[offsets[0]])
    depth = trail.shape[1]
    planes = lax.axis_size("col") // 2
    rows = trail.shape[0] // (2 * planes)
    at = jnp.stack([offset, core]).astype(jnp.int32)
    return pl.pallas_call(
        functools.partial(times_trail_kernel, offsets, counts),
        out_shape=jax.ShapeDtypeStruct((planes, width, rows), jnp.float32),
        grid_spec=pltpu.PrefetchScalarGridSpec(
            num_scalar_prefetch=1,
            grid=(planes,),
            in_specs=[pl.BlockSpec(piece.shape, lambda j, at: (0, 0)) for piece in pieces]
            + [pl.BlockSpec((rows, depth), lambda j, at: (2 * j + at[1], 0))]
            + [pl.BlockSpec(memory_space=pl.ANY)] * len(after),
            out_specs=pl.BlockSpec((1, width, rows), lambda j, at: (j, 0, 0)),
            scratch_shapes=[
                pltpu.VMEM((width, depth), jnp.float32),
                pltpu.VMEM((2 * width, depth), jnp.bfloat16),
            ],
        ),
        compiler_params=pltpu.CompilerParams(vmem_limit_bytes=VMEM_LIMIT),
        cost_estimate=cost(weight * 8.6 * width * depth * rows * planes),
    )(at, *pieces, trail, *after)


def sum_over_planes(block):
    planes, width, rows = block.shape
    groups = [[2 * plane + core for plane in range(planes)] for core in range(2)]
    return lax.psum_scatter(
        block.reshape(planes * width, rows),
        "col",
        scatter_dimension=0,
        tiled=True,
        axis_index_groups=groups,
    )


def pick(blocks, which):
    return lax.dynamic_index_in_dim(blocks, which, 0, keepdims=False)


def swap(block, axis, offset):
    return lax.ppermute(block, axis, [(i, i ^ offset) for i in range(lax.axis_size(axis))])


def exchange_order():
    order = [("col", 1)]
    order += [("row", 1 << b) for b in range(lax.axis_size("row").bit_length() - 1)]
    order += [("col", 1 << b) for b in range(1, lax.axis_size("col").bit_length() - 1)]
    return order


def sum_shares(block, least, order, halved=()):
    halved = list(halved)
    for axis, bit in order:
        rows = block.shape[0]
        if rows // 2 >= least and rows % 16 == 0:
            upper = (lax.axis_index(axis) & bit) != 0
            low, high = block[: rows // 2], block[rows // 2 :]
            block = jnp.where(upper, high, low) + swap(jnp.where(upper, low, high), axis, bit)
            halved.append((axis, bit, upper))
        else:
            block = block + swap(block, axis, bit)
    return block, halved


def join_shares(block, halved):
    for axis, bit, upper in reversed(halved):
        other = swap(block, axis, bit)
        block = jnp.concatenate([jnp.where(upper, other, block), jnp.where(upper, block, other)], 0)
    return block


def slot_table(row_owners):
    table = []
    for row in range(row_owners):
        rest = [row ^ (1 << b) for b in range(row_owners.bit_length() - 1)]
        second = max(rest)
        others = [c for c in range(row_owners - 1, -1, -1) if c not in (row, second)]
        table.append([row, second] + others)
    return np.array(table)


def per_device(trail_grad, factor_rows, factor_top, rows_grad, top_grad):
    row_owner = lax.axis_index("row")
    row_owners = lax.axis_size("row")
    core = lax.axis_index("col") % 2
    panel_width = factor_top.shape[0]
    chunk = factor_rows.shape[1]
    own_rows = rows_grad.shape[0]
    table = slot_table(row_owners)
    late = len(set(table[:, -1]))
    split = late * chunk
    whiches = [jnp.asarray(table[:, slot])[row_owner] for slot in range(row_owners)]

    own_panel = factor_rows.T
    stay, go = pack_panel(own_panel)
    arrived = swap(go, "col", 1)
    panels = neighbour_panels(own_panel)

    aligned = None

    def multiply(slot, after):
        nonlocal aligned
        offset = whiches[slot] ^ row_owner
        offsets = sorted({int(table[r, slot]) ^ r for r in range(row_owners)})
        candidates = {each: panels[each] for each in offsets}
        theirs = times_trail(candidates, offset, 1 - core, trail_grad, WEIGHTS[min(slot, 2)], after)
        between = (ahead,) if slot == 0 else ()
        if slot == row_owners - 1:
            aligned = place_rows(spread, (theirs,))
            between = (aligned,)
        ours = times_trail(
            candidates, offset, core, trail_grad, WEIGHTS[min(slot, 2)], (theirs, *between)
        )
        half = theirs.shape[0] // 2
        if slot == 1 and half:
            theirs = [swap(theirs[:half], "col", 1), swap(theirs[half:], "col", 1)]
            theirs = jnp.concatenate(theirs, 0)
        else:
            theirs = swap(theirs, "col", 1)
        total = ours + theirs
        return sum_over_planes(total), total

    def settle(slot, after=()):
        shapes = [
            jax.ShapeDtypeStruct((chunk, own_rows), jnp.float32),
            jax.ShapeDtypeStruct((chunk, panel_width), jnp.float32),
        ]
        return whole_in_vmem(
            settle_kernel,
            shapes,
            [],
            [waiting[slot], grads, aligned],
            1024,
            scalars=jnp.full((1,), whiches[slot], jnp.int32),
            after=after,
        )

    planes = stay.shape[0]
    first = planes // 2
    ahead = swap(jnp.stack([stay[first], arrived[first]]), "col", 2 * first)
    summed, done = multiply(0, (arrived,))
    waiting = [summed]
    near = [panels[offset][0] for offset in panels if offset]
    later, pairs = stage(own_panel, stay, arrived, (done, *near))
    for offset in range(1, row_owners):
        if offset not in panels:
            panels[offset] = [swap(later, "row", offset)]
    pairs = [
        pairs[0] if j == 0 else ahead if j == first else swap(pairs[j], "col", 2 * j)
        for j in range(planes)
    ]
    done = later
    for slot in range(1, row_owners):
        if slot == 2:
            grads = done = whole_in_vmem(
                turn_kernel,
                jax.ShapeDtypeStruct((row_owners, chunk, own_rows), jnp.float32),
                [],
                [rows_grad],
                1024,
                after=(done,),
            )
        if slot == row_owners - 1:
            spread, done = align_rows(pairs, (done, waiting[0]))
        before = (waiting[slot - 2],) if slot >= 3 else ()
        summed, done = multiply(slot, (done, *before))
        waiting.append(summed)
    rests, inner = [], []

    def adjoint_rows(slots, known=()):
        return whole_in_vmem(
            adjoint_kernel,
            jax.ShapeDtypeStruct((own_rows, panel_width), jnp.float32),
            [],
            [inverse.reshape(row_owners, chunk, panel_width), *(rests[slot] for slot in slots), *known],
            1024,
            scalars=jnp.stack([whiches[slot] for slot in slots]).astype(jnp.int32),
        )

    for slot in range(row_owners - 1):
        rest, part = settle(slot, (done,))
        done = part
        rests.append(rest)
        inner.append(part)
    inverse = triangular_inverse(factor_top, (done,))
    adjoint = adjoint_rows(range(row_owners - 1))
    early = jnp.concatenate(
        [
            sum(jnp.where(whiches[s] == each, inner[s], 0.0) for s in range(row_owners - 1))
            for each in range(late, row_owners)
        ],
        0,
    )
    order = exchange_order()
    share, halved = sum_shares(early, 8, order[:STEPS])
    rest, part = settle(row_owners - 1, (adjoint,))
    rests.append(rest)
    share = whole_in_vmem(
        copy_kernel,
        jax.ShapeDtypeStruct(share.shape, jnp.float32),
        [],
        [share],
        1024,
        after=(part,),
    )
    early = join_shares(*sum_shares(share, 8, order[STEPS:], halved))
    inner.append(part)
    adjoint = adjoint_rows([row_owners - 1], [adjoint])
    last = jnp.concatenate(
        [
            sum(jnp.where(whiches[s] == each, inner[s][:, :split], 0.0) for s in range(row_owners))
            for each in range(late)
        ],
        0,
    )
    last = join_shares(*sum_shares(last, 64, order))

    lo, hi = slice(0, split), slice(split, panel_width)
    rest = panel_width - split
    out_hi, out_mix, base = whole_in_vmem(
        early_kernel,
        [jax.ShapeDtypeStruct(each, jnp.float32) for each in ((rest, rest), (rest, split), (split, split))],
        [],
        [
            early,
            inverse[hi, hi],
            inverse[lo, lo],
            factor_top[hi, hi],
            factor_top[hi, lo],
            top_grad[hi, hi],
            top_grad[hi, lo],
            top_grad[lo, lo],
        ],
        36 * panel_width**3,
    )
    out_lo = whole_in_vmem(
        last_kernel,
        jax.ShapeDtypeStruct((split, split), jnp.float32),
        [],
        [last, inverse[lo, lo], factor_top[lo, lo], base],
        14 * panel_width**3,
    )
    top_out = jnp.concatenate(
        [
            jnp.concatenate([out_lo, jnp.zeros((split, rest), jnp.float32)], 1),
            jnp.concatenate([out_mix, out_hi], 1),
        ],
        0,
    )
    return adjoint, top_out


def solution(mesh):
    placed = (P("row", "col"), P("col", "row"), P(), P(("row", "col"), None), P())
    return jax.shard_map(
        per_device,
        mesh=mesh,
        in_specs=placed,
        out_specs=(P(("row", "col"), None), P()),
        check_vma=False,
    )
```

```python
import functools

import jax
import jax.numpy as jnp
import numpy as np
from jax import lax
from jax.experimental import pallas as pl
from jax.experimental.pallas import tpu as pltpu
from jax.sharding import PartitionSpec as P

NB = 256
NP = 3
CB = 128
LEAF = 32
STEPS = 4
VMEM_LIMIT = 48 * 1024 * 1024
WEIGHTS = (4.0, 0.4, 2.0)

exact_dots = lax.Precision.HIGHEST
split_dots = lax.Precision.HIGH


def dims_dot(left, right, left_dim, right_dim, precision=exact_dots):
    return lax.dot_general(
        left,
        right,
        (((left_dim,), (right_dim,)), ((), ())),
        precision=precision,
        preferred_element_type=jnp.float32,
    )


def product(left, right):
    return dims_dot(left, right, 1, 0)


def lower_half(matrix):
    row_ids = lax.broadcasted_iota(jnp.int32, matrix.shape, 0)
    col_ids = lax.broadcasted_iota(jnp.int32, matrix.shape, 1)
    return jnp.where(row_ids > col_ids, matrix, jnp.where(row_ids == col_ids, 0.5 * matrix, 0.0))


def inverse_kernel(factor_ref, out_ref, spread_ref, leaf_out):
    width = factor_ref.shape[0]
    dot = functools.partial(jnp.dot, precision=exact_dots, preferred_element_type=jnp.float32)
    rows = lax.broadcasted_iota(jnp.int32, (CB, CB), 0)
    cols = lax.broadcasted_iota(jnp.int32, (CB, CB), 1)
    same_leaf = rows // LEAF == cols // LEAF
    ones = jnp.where(same_leaf, 1.0, 0.0)
    lane_at = lax.broadcasted_iota(jnp.int32, (LEAF, CB), 1) % LEAF
    for at in range(0, width, CB):
        turned = jnp.where(same_leaf, factor_ref[at : at + CB, at : at + CB], 0.0).T
        leaves = sum(turned[low : low + LEAF] for low in range(0, CB, LEAF))
        picked = jnp.concatenate(
            [jnp.where(lane_at == row, leaves, 0.0) for row in range(LEAF)], 0
        )
        spread_ref[:, at : at + CB] = dot(picked, ones)
    lane = lax.broadcasted_iota(jnp.int32, (1, width), 1) % LEAF
    row_at = lax.broadcasted_iota(jnp.int32, (LEAF, width), 0)
    leaf_out[...] = jnp.zeros_like(leaf_out)
    for row in range(LEAF):
        known = spread_ref[row * LEAF : (row + 1) * LEAF]
        diag = known[row : row + 1]
        total = jnp.sum(jnp.where(row_at < row, known * leaf_out[...], 0.0), axis=0, keepdims=True)
        leaf_out[row : row + 1] = (jnp.where(lane == row, 1.0, 0.0) - total) / diag
    out_ref[...] = jnp.zeros_like(out_ref)
    for at in range(0, width, CB):
        spread = jnp.concatenate([leaf_out[:, at : at + CB]] * (CB // LEAF), 0)
        inv = jnp.where(same_leaf, spread, 0.0)
        block = factor_ref[at : at + CB, at : at + CB]
        size = LEAF
        while size < CB:
            below = (rows // size == cols // size + 1) & (rows // (2 * size) == cols // (2 * size))
            inv = inv - dot(dot(inv, jnp.where(below, block, 0.0)), inv)
            size *= 2
        out_ref[at : at + CB, at : at + CB] = inv
    for at in range(0, width, NB):
        size = CB
        while size < NB:
            for low in range(at, at + NB, 2 * size):
                mid, high = low + size, low + 2 * size
                first = out_ref[low:mid, low:mid]
                second = out_ref[mid:high, mid:high]
                out_ref[mid:high, low:mid] = -dot(dot(second, factor_ref[mid:high, low:mid]), first)
            size *= 2
    for at in range(NB, width, NB):
        carried = dot(factor_ref[at : at + NB, :at], out_ref[:at, :at])
        out_ref[at : at + NB, :at] = -dot(out_ref[at : at + NB, at : at + NB], carried)


def cost(flops):
    return pl.CostEstimate(flops=int(flops), bytes_accessed=1024, transcendentals=0)


def whole_in_vmem(kernel, out_shape, scratch, operands, flops, scalars=None, after=()):
    first = () if scalars is None else (scalars,)

    def body(*refs):
        head = refs[: len(first)]
        inputs = refs[len(first) : len(first) + len(operands)]
        rest = refs[len(first) + len(operands) + len(after) :]
        kernel(*head, *inputs, *rest)

    return pl.pallas_call(
        body,
        out_shape=out_shape,
        in_specs=[pl.BlockSpec(memory_space=pltpu.SMEM)] * len(first)
        + [pl.BlockSpec(memory_space=pltpu.VMEM)] * len(operands)
        + [pl.BlockSpec(memory_space=pl.ANY)] * len(after),
        out_specs=jax.tree.map(lambda _: pl.BlockSpec(memory_space=pltpu.VMEM), out_shape),
        scratch_shapes=scratch,
        compiler_params=pltpu.CompilerParams(vmem_limit_bytes=VMEM_LIMIT),
        cost_estimate=cost(flops),
    )(*first, *operands, *after)


def triangular_inverse(factor, after):
    width = factor.shape[0]
    return whole_in_vmem(
        inverse_kernel,
        jax.ShapeDtypeStruct((width, width), jnp.float32),
        [pltpu.VMEM((LEAF * LEAF, width), jnp.float32), pltpu.VMEM((LEAF, width), jnp.float32)],
        [factor],
        1024,
        after=after,
    )


def halves(matrix):
    high = matrix.astype(jnp.bfloat16)
    return high, (matrix - high.astype(jnp.float32)).astype(jnp.bfloat16)


def split_product(left, right):
    left_high, left_low = halves(left)
    right_high, right_low = halves(right)
    small = dims_dot(left_low, right_high, 1, 0, None) + dims_dot(left_high, right_low, 1, 0, None)
    return dims_dot(left_high, right_high, 1, 0, None) + small


def turned_split(left, right):
    return split_product(left.T, right)


def turned_product(left, right):
    return product(left.T, right)


def early_kernel(inner, inv_hi, inv_lo, fac_hi, fac_mix, top_hi, top_mix, top_lo, out_hi, out_mix, base):
    split = inv_lo.shape[0]
    turned = inv_hi[...].T
    moved = split_product(turned, inner[...])
    lower = jnp.tril(top_hi[...] - moved[:, split:])
    middle = lower_half(turned_split(fac_hi[...], lower))
    whole = split_product(split_product(turned, middle), inv_hi[...])
    whole = whole + whole.T
    out_hi[...] = lower_half(whole)
    moved = moved[:, :split]
    mixed = split_product(top_mix[...] - moved - split_product(whole, fac_mix[...]), inv_lo[...])
    out_mix[...] = mixed
    known = turned_split(inv_lo[...], turned_split(fac_mix[...], moved))
    base[...] = top_lo[...] + known - turned_split(mixed, fac_mix[...])


def last_kernel(inner, inv, fac, base, result):
    turned = inv[...].T
    lower = jnp.tril(base[...] - split_product(turned, inner[...]))
    middle = lower_half(turned_split(fac[...], lower))
    whole = split_product(split_product(turned, middle), inv[...])
    result[...] = lower_half(whole + whole.T)


def pack_kernel(at_ref, first_ref, second_ref, stay_ref, go_ref):
    stay_ref[0] = first_ref[...]
    go_ref[0] = second_ref[...]


def pack_panel(panel, after=()):
    width, owned = panel.shape
    owners = lax.axis_size("col")
    part = owned // owners
    here = lax.axis_index("col")
    if part % CB:
        blocks = panel.reshape(width, owners, part).transpose(1, 0, 2)
        blocks = jnp.take(blocks, jnp.arange(owners) ^ here, axis=0)
        return blocks[0::2], blocks[1::2]
    shape = jax.ShapeDtypeStruct((owners // 2, width, part), jnp.float32)
    out_spec = pl.BlockSpec((1, width, part), lambda j, at: (j, 0, 0))
    return pl.pallas_call(
        pack_kernel,
        out_shape=(shape, shape),
        grid_spec=pltpu.PrefetchScalarGridSpec(
            num_scalar_prefetch=1,
            grid=(owners // 2,),
            in_specs=[
                pl.BlockSpec((width, part), lambda j, at: (0, (2 * j) ^ at[0])),
                pl.BlockSpec((width, part), lambda j, at: (0, (2 * j + 1) ^ at[0])),
            ],
            out_specs=(out_spec, out_spec),
        ),
        compiler_params=pltpu.CompilerParams(vmem_limit_bytes=VMEM_LIMIT),
        cost_estimate=cost(8 * 256 * panel.size),
    )(jnp.full((1,), here, jnp.int32), panel, panel)


def regroup_kernel(tile, at_ref, *refs):
    pairs, out_ref, blocks_ref = refs[:-2], refs[-2], refs[-1]
    owners, _, part = blocks_ref.shape
    rows = out_ref.shape[0]
    for j, pair in enumerate(pairs):
        blocks_ref[2 * j] = pair[0]
        blocks_ref[2 * j + 1] = pair[1]
    for offset in range(rows):
        lane = 0
        for q in range(0, part, tile):
            for group in range(owners // rows):
                source = (at_ref[0] ^ offset) + rows * (group ^ at_ref[1])
                out_ref[offset, :, lane : lane + tile] = blocks_ref[source, :, q : q + tile]
                lane += tile


def place_kernel(at_ref, *refs):
    pieces, out_ref = refs[:-1], refs[-1]
    for offset, piece in enumerate(pieces):
        out_ref[at_ref[0] ^ offset] = piece[...]


def align_rows(pairs, after):
    width, part = pairs[0].shape[1:]
    owners = 2 * len(pairs)
    row_owners = lax.axis_size("row")
    here = lax.axis_index("col")
    row = lax.axis_index("row")
    rows = part * owners // row_owners
    at = jnp.stack([(here % row_owners) ^ row, here // row_owners]).astype(jnp.int32)
    grouped = whole_in_vmem(
        functools.partial(regroup_kernel, min(CB, part)),
        jax.ShapeDtypeStruct((row_owners, width, rows), jnp.float32),
        [pltpu.VMEM((owners, width, part), jnp.float32)],
        pairs,
        4 * 256 * owners * width * part,
        scalars=at,
        after=after,
    )
    arrived = [grouped[0]]
    arrived += [swap(grouped[offset], "row", offset) for offset in range(1, row_owners)]
    return arrived, grouped


def place_rows(arrived, after):
    row_owners = len(arrived)
    width, rows = arrived[0].shape
    aligned = whole_in_vmem(
        place_kernel,
        jax.ShapeDtypeStruct((row_owners, width, rows), jnp.float32),
        [],
        arrived,
        1024,
        scalars=jnp.full((1,), lax.axis_index("row"), jnp.int32),
        after=after,
    )
    return aligned.reshape(row_owners * width, rows)


def turn_kernel(source, target):
    turned = source[...].T
    chunk = target.shape[1]
    for at in range(target.shape[0]):
        target[at] = turned[at * chunk : (at + 1) * chunk]


def settle_kernel(at_ref, summed, grads, aligned, rest_out, inner_out):
    rest = grads[at_ref[0]] - 2.0 * summed[...]
    rest_out[...] = rest
    inner_out[...] = dims_dot(rest, aligned[...], 1, 1)


def adjoint_kernel(at_ref, inverse, *refs):
    count = at_ref.shape[0]
    rests, known, target = refs[:count], refs[count:-1], refs[-1]
    total = sum(each[...] for each in known)
    for slot, rest in enumerate(rests):
        total += turned_product(rest[...], inverse[at_ref[slot]])
    target[...] = total


def neighbour_panels(panel):
    bits = lax.axis_size("row").bit_length() - 1
    return {0: [panel]} | {1 << b: [swap(panel, "row", 1 << b)] for b in range(bits)}


def copy_kernel(source, target):
    target[...] = source[...]


def stage_kernel(panel, stay, arrived, later, *pairs):
    later[...] = panel[...]
    for j, pair in enumerate(pairs):
        pair[0] = stay[j]
        pair[1] = arrived[j]


def stage(panel, stay, arrived, after):
    shapes = [jax.ShapeDtypeStruct(panel.shape, jnp.float32)]
    shapes += [jax.ShapeDtypeStruct((2,) + stay.shape[1:], jnp.float32)] * stay.shape[0]
    later, *pairs = whole_in_vmem(
        stage_kernel, shapes, [], [panel, stay, arrived], 8 * 256 * panel.size, after=after
    )
    return later, pairs


def times_trail_kernel(offsets, counts, at_ref, *refs):
    panel_refs, trail_ref = refs[: sum(counts)], refs[sum(counts)]
    out_ref, panel_at, halves_at = refs[-3:]

    @pl.when(pl.program_id(0) == 0)
    def _():
        first = 0
        for offset, count in zip(offsets, counts):
            pieces = panel_refs[first : first + count]
            first += count

            @pl.when(at_ref[0] == offset)
            def _():
                row = 0
                for piece in pieces:
                    panel_at[row : row + piece.shape[0]] = piece[...]
                    row += piece.shape[0]

        panel = panel_at[...]
        high = panel.astype(jnp.bfloat16)
        halves_at[: panel.shape[0]] = high
        halves_at[panel.shape[0] :] = (panel - high.astype(jnp.float32)).astype(jnp.bfloat16)

    width = panel_at.shape[0]
    depth = trail_ref.shape[1]
    step = min(depth, 2 * NB)
    total = jnp.zeros(out_ref.shape[1:], jnp.float32)
    for k in range(0, depth, step):
        trail = trail_ref[:, k : k + step]
        high = trail.astype(jnp.bfloat16)
        low = (trail - high.astype(jnp.float32)).astype(jnp.bfloat16)
        both = dims_dot(halves_at[:, k : k + step], high, 1, 1, None)
        total += both[:width] + both[width:]
        total += dims_dot(halves_at[:width, k : k + step], low, 1, 1, None)
    out_ref[0] = total


def times_trail(candidates, offset, core, trail, weight, after=()):
    offsets = tuple(candidates)
    counts = tuple(len(candidates[each]) for each in offsets)
    pieces = [piece for each in offsets for piece in candidates[each]]
    width = sum(piece.shape[0] for piece in candidates[offsets[0]])
    depth = trail.shape[1]
    planes = lax.axis_size("col") // 2
    rows = trail.shape[0] // (2 * planes)
    at = jnp.stack([offset, core]).astype(jnp.int32)
    return pl.pallas_call(
        functools.partial(times_trail_kernel, offsets, counts),
        out_shape=jax.ShapeDtypeStruct((planes, width, rows), jnp.float32),
        grid_spec=pltpu.PrefetchScalarGridSpec(
            num_scalar_prefetch=1,
            grid=(planes,),
            in_specs=[pl.BlockSpec(piece.shape, lambda j, at: (0, 0)) for piece in pieces]
            + [pl.BlockSpec((rows, depth), lambda j, at: (2 * j + at[1], 0))]
            + [pl.BlockSpec(memory_space=pl.ANY)] * len(after),
            out_specs=pl.BlockSpec((1, width, rows), lambda j, at: (j, 0, 0)),
            scratch_shapes=[
                pltpu.VMEM((width, depth), jnp.float32),
                pltpu.VMEM((2 * width, depth), jnp.bfloat16),
            ],
        ),
        compiler_params=pltpu.CompilerParams(vmem_limit_bytes=VMEM_LIMIT),
        cost_estimate=cost(weight * 8.6 * width * depth * rows * planes),
    )(at, *pieces, trail, *after)


def sum_over_planes(block):
    planes, width, rows = block.shape
    groups = [[2 * plane + core for plane in range(planes)] for core in range(2)]
    return lax.psum_scatter(
        block.reshape(planes * width, rows),
        "col",
        scatter_dimension=0,
        tiled=True,
        axis_index_groups=groups,
    )


def pick(blocks, which):
    return lax.dynamic_index_in_dim(blocks, which, 0, keepdims=False)


def swap(block, axis, offset):
    return lax.ppermute(block, axis, [(i, i ^ offset) for i in range(lax.axis_size(axis))])


def exchange_order():
    order = [("col", 1)]
    order += [("row", 1 << b) for b in range(lax.axis_size("row").bit_length() - 1)]
    order += [("col", 1 << b) for b in range(1, lax.axis_size("col").bit_length() - 1)]
    return order


def sum_shares(block, least, order, halved=()):
    halved = list(halved)
    for axis, bit in order:
        rows = block.shape[0]
        if rows // 2 >= least and rows % 16 == 0:
            upper = (lax.axis_index(axis) & bit) != 0
            low, high = block[: rows // 2], block[rows // 2 :]
            block = jnp.where(upper, high, low) + swap(jnp.where(upper, low, high), axis, bit)
            halved.append((axis, bit, upper))
        else:
            block = block + swap(block, axis, bit)
    return block, halved


def join_shares(block, halved):
    for axis, bit, upper in reversed(halved):
        other = swap(block, axis, bit)
        block = jnp.concatenate([jnp.where(upper, other, block), jnp.where(upper, block, other)], 0)
    return block


def slot_table(row_owners):
    table = []
    for row in range(row_owners):
        rest = [row ^ (1 << b) for b in range(row_owners.bit_length() - 1)]
        second = max(rest)
        others = [c for c in range(row_owners - 1, -1, -1) if c not in (row, second)]
        table.append([row, second] + others)
    return np.array(table)


def per_device(trail_grad, factor_rows, factor_top, rows_grad, top_grad):
    row_owner = lax.axis_index("row")
    row_owners = lax.axis_size("row")
    core = lax.axis_index("col") % 2
    panel_width = factor_top.shape[0]
    chunk = factor_rows.shape[1]
    own_rows = rows_grad.shape[0]
    table = slot_table(row_owners)
    late = len(set(table[:, -1]))
    split = late * chunk
    whiches = [jnp.asarray(table[:, slot])[row_owner] for slot in range(row_owners)]

    own_panel = factor_rows.T
    stay, go = pack_panel(own_panel)
    arrived = swap(go, "col", 1)
    panels = neighbour_panels(own_panel)

    aligned = None

    def multiply(slot, after):
        nonlocal aligned
        offset = whiches[slot] ^ row_owner
        offsets = sorted({int(table[r, slot]) ^ r for r in range(row_owners)})
        candidates = {each: panels[each] for each in offsets}
        theirs = times_trail(candidates, offset, 1 - core, trail_grad, WEIGHTS[min(slot, 2)], after)
        between = (ahead,) if slot == 0 else ()
        if slot == row_owners - 1:
            aligned = place_rows(spread, (theirs,))
            between = (aligned,)
        ours = times_trail(
            candidates, offset, core, trail_grad, WEIGHTS[min(slot, 2)], (theirs, *between)
        )
        half = theirs.shape[0] // 2
        if slot == 1 and half:
            theirs = [swap(theirs[:half], "col", 1), swap(theirs[half:], "col", 1)]
            theirs = jnp.concatenate(theirs, 0)
        else:
            theirs = swap(theirs, "col", 1)
        total = ours + theirs
        return sum_over_planes(total), total

    def settle(slot, after=()):
        shapes = [
            jax.ShapeDtypeStruct((chunk, own_rows), jnp.float32),
            jax.ShapeDtypeStruct((chunk, panel_width), jnp.float32),
        ]
        return whole_in_vmem(
            settle_kernel,
            shapes,
            [],
            [waiting[slot], grads, aligned],
            1024,
            scalars=jnp.full((1,), whiches[slot], jnp.int32),
            after=after,
        )

    planes = stay.shape[0]
    first = planes // 2
    ahead = swap(jnp.stack([stay[first], arrived[first]]), "col", 2 * first)
    summed, done = multiply(0, (arrived,))
    waiting = [summed]
    near = [panels[offset][0] for offset in panels if offset]
    later, pairs = stage(own_panel, stay, arrived, (done, *near))
    for offset in range(1, row_owners):
        if offset not in panels:
            panels[offset] = [swap(later, "row", offset)]
    pairs = [
        pairs[0] if j == 0 else ahead if j == first else swap(pairs[j], "col", 2 * j)
        for j in range(planes)
    ]
    done = later
    for slot in range(1, row_owners):
        if slot == 2:
            inverse = triangular_inverse(factor_top, (done,))
            grads = done = whole_in_vmem(
                turn_kernel,
                jax.ShapeDtypeStruct((row_owners, chunk, own_rows), jnp.float32),
                [],
                [rows_grad],
                1024,
                after=(inverse,),
            )
        if slot == row_owners - 1:
            spread, done = align_rows(pairs, (done, waiting[0]))
        before = (waiting[slot - 2],) if slot >= 3 else ()
        summed, done = multiply(slot, (done, *before))
        waiting.append(summed)
    rests, inner = [], []

    def adjoint_rows(slots, known=()):
        return whole_in_vmem(
            adjoint_kernel,
            jax.ShapeDtypeStruct((own_rows, panel_width), jnp.float32),
            [],
            [inverse.reshape(row_owners, chunk, panel_width), *(rests[slot] for slot in slots), *known],
            1024,
            scalars=jnp.stack([whiches[slot] for slot in slots]).astype(jnp.int32),
        )

    for slot in range(row_owners - 1):
        rest, part = settle(slot, (done,))
        done = part
        rests.append(rest)
        inner.append(part)
    adjoint = adjoint_rows(range(row_owners - 1))
    early = jnp.concatenate(
        [
            sum(jnp.where(whiches[s] == each, inner[s], 0.0) for s in range(row_owners - 1))
            for each in range(late, row_owners)
        ],
        0,
    )
    order = exchange_order()
    share, halved = sum_shares(early, 8, order[:STEPS])
    rest, part = settle(row_owners - 1, (adjoint,))
    rests.append(rest)
    share = whole_in_vmem(
        copy_kernel,
        jax.ShapeDtypeStruct(share.shape, jnp.float32),
        [],
        [share],
        1024,
        after=(part,),
    )
    early = join_shares(*sum_shares(share, 8, order[STEPS:], halved))
    inner.append(part)
    adjoint = adjoint_rows([row_owners - 1], [adjoint])
    last = jnp.concatenate(
        [
            sum(jnp.where(whiches[s] == each, inner[s][:, :split], 0.0) for s in range(row_owners))
            for each in range(late)
        ],
        0,
    )
    last = join_shares(*sum_shares(last, 64, order))

    lo, hi = slice(0, split), slice(split, panel_width)
    rest = panel_width - split
    out_hi, out_mix, base = whole_in_vmem(
        early_kernel,
        [jax.ShapeDtypeStruct(each, jnp.float32) for each in ((rest, rest), (rest, split), (split, split))],
        [],
        [
            early,
            inverse[hi, hi],
            inverse[lo, lo],
            factor_top[hi, hi],
            factor_top[hi, lo],
            top_grad[hi, hi],
            top_grad[hi, lo],
            top_grad[lo, lo],
        ],
        36 * panel_width**3,
    )
    out_lo = whole_in_vmem(
        last_kernel,
        jax.ShapeDtypeStruct((split, split), jnp.float32),
        [],
        [last, inverse[lo, lo], factor_top[lo, lo], base],
        14 * panel_width**3,
    )
    top_out = jnp.concatenate(
        [
            jnp.concatenate([out_lo, jnp.zeros((split, rest), jnp.float32)], 1),
            jnp.concatenate([out_mix, out_hi], 1),
        ],
        0,
    )
    return adjoint, top_out


def solution(mesh):
    placed = (P("row", "col"), P("col", "row"), P(), P(("row", "col"), None), P())
    return jax.shard_map(
        per_device,
        mesh=mesh,
        in_specs=placed,
        out_specs=(P(("row", "col"), None), P()),
        check_vma=False,
    )
```

```python
import functools

import jax
import jax.numpy as jnp
import numpy as np
from jax import lax
from jax.experimental import pallas as pl
from jax.experimental.pallas import tpu as pltpu
from jax.sharding import PartitionSpec as P

NB = 256
NP = 3
CB = 128
LEAF = 32
STEPS = 3
VMEM_LIMIT = 48 * 1024 * 1024
WEIGHTS = (4.0, 0.4, 2.0)

exact_dots = lax.Precision.HIGHEST
split_dots = lax.Precision.HIGH


def dims_dot(left, right, left_dim, right_dim, precision=exact_dots):
    return lax.dot_general(
        left,
        right,
        (((left_dim,), (right_dim,)), ((), ())),
        precision=precision,
        preferred_element_type=jnp.float32,
    )


def product(left, right):
    return dims_dot(left, right, 1, 0)


def lower_half(matrix):
    row_ids = lax.broadcasted_iota(jnp.int32, matrix.shape, 0)
    col_ids = lax.broadcasted_iota(jnp.int32, matrix.shape, 1)
    return jnp.where(row_ids > col_ids, matrix, jnp.where(row_ids == col_ids, 0.5 * matrix, 0.0))


def inverse_kernel(factor_ref, out_ref, spread_ref, leaf_out):
    width = factor_ref.shape[0]
    dot = functools.partial(jnp.dot, precision=exact_dots, preferred_element_type=jnp.float32)
    rows = lax.broadcasted_iota(jnp.int32, (CB, CB), 0)
    cols = lax.broadcasted_iota(jnp.int32, (CB, CB), 1)
    same_leaf = rows // LEAF == cols // LEAF
    ones = jnp.where(same_leaf, 1.0, 0.0)
    lane_at = lax.broadcasted_iota(jnp.int32, (LEAF, CB), 1) % LEAF
    for at in range(0, width, CB):
        turned = jnp.where(same_leaf, factor_ref[at : at + CB, at : at + CB], 0.0).T
        leaves = sum(turned[low : low + LEAF] for low in range(0, CB, LEAF))
        picked = jnp.concatenate(
            [jnp.where(lane_at == row, leaves, 0.0) for row in range(LEAF)], 0
        )
        spread_ref[:, at : at + CB] = dot(picked, ones)
    lane = lax.broadcasted_iota(jnp.int32, (1, width), 1) % LEAF
    row_at = lax.broadcasted_iota(jnp.int32, (LEAF, width), 0)
    leaf_out[...] = jnp.zeros_like(leaf_out)
    for row in range(LEAF):
        known = spread_ref[row * LEAF : (row + 1) * LEAF]
        diag = known[row : row + 1]
        total = jnp.sum(jnp.where(row_at < row, known * leaf_out[...], 0.0), axis=0, keepdims=True)
        leaf_out[row : row + 1] = (jnp.where(lane == row, 1.0, 0.0) - total) / diag
    out_ref[...] = jnp.zeros_like(out_ref)
    for at in range(0, width, CB):
        spread = jnp.concatenate([leaf_out[:, at : at + CB]] * (CB // LEAF), 0)
        inv = jnp.where(same_leaf, spread, 0.0)
        block = factor_ref[at : at + CB, at : at + CB]
        size = LEAF
        while size < CB:
            below = (rows // size == cols // size + 1) & (rows // (2 * size) == cols // (2 * size))
            inv = inv - dot(dot(inv, jnp.where(below, block, 0.0)), inv)
            size *= 2
        out_ref[at : at + CB, at : at + CB] = inv
    for at in range(0, width, NB):
        size = CB
        while size < NB:
            for low in range(at, at + NB, 2 * size):
                mid, high = low + size, low + 2 * size
                first = out_ref[low:mid, low:mid]
                second = out_ref[mid:high, mid:high]
                out_ref[mid:high, low:mid] = -dot(dot(second, factor_ref[mid:high, low:mid]), first)
            size *= 2
    for at in range(NB, width, NB):
        carried = dot(factor_ref[at : at + NB, :at], out_ref[:at, :at])
        out_ref[at : at + NB, :at] = -dot(out_ref[at : at + NB, at : at + NB], carried)


def cost(flops):
    return pl.CostEstimate(flops=int(flops), bytes_accessed=1024, transcendentals=0)


def whole_in_vmem(kernel, out_shape, scratch, operands, flops, scalars=None, after=()):
    first = () if scalars is None else (scalars,)

    def body(*refs):
        head = refs[: len(first)]
        inputs = refs[len(first) : len(first) + len(operands)]
        rest = refs[len(first) + len(operands) + len(after) :]
        kernel(*head, *inputs, *rest)

    return pl.pallas_call(
        body,
        out_shape=out_shape,
        in_specs=[pl.BlockSpec(memory_space=pltpu.SMEM)] * len(first)
        + [pl.BlockSpec(memory_space=pltpu.VMEM)] * len(operands)
        + [pl.BlockSpec(memory_space=pl.ANY)] * len(after),
        out_specs=jax.tree.map(lambda _: pl.BlockSpec(memory_space=pltpu.VMEM), out_shape),
        scratch_shapes=scratch,
        compiler_params=pltpu.CompilerParams(vmem_limit_bytes=VMEM_LIMIT),
        cost_estimate=cost(flops),
    )(*first, *operands, *after)


def triangular_inverse(factor, after):
    width = factor.shape[0]
    return whole_in_vmem(
        inverse_kernel,
        jax.ShapeDtypeStruct((width, width), jnp.float32),
        [pltpu.VMEM((LEAF * LEAF, width), jnp.float32), pltpu.VMEM((LEAF, width), jnp.float32)],
        [factor],
        1024,
        after=after,
    )


def halves(matrix):
    high = matrix.astype(jnp.bfloat16)
    return high, (matrix - high.astype(jnp.float32)).astype(jnp.bfloat16)


def split_product(left, right):
    left_high, left_low = halves(left)
    right_high, right_low = halves(right)
    small = dims_dot(left_low, right_high, 1, 0, None) + dims_dot(left_high, right_low, 1, 0, None)
    return dims_dot(left_high, right_high, 1, 0, None) + small


def turned_split(left, right):
    return split_product(left.T, right)


def early_kernel(inner, inv_hi, inv_lo, fac_hi, fac_mix, top_hi, top_mix, top_lo, out_hi, out_mix, base):
    split = inv_lo.shape[0]
    turned = inv_hi[...].T
    moved = split_product(turned, inner[...])
    lower = jnp.tril(top_hi[...] - moved[:, split:])
    middle = lower_half(turned_split(fac_hi[...], lower))
    whole = split_product(split_product(turned, middle), inv_hi[...])
    whole = whole + whole.T
    out_hi[...] = lower_half(whole)
    moved = moved[:, :split]
    mixed = split_product(top_mix[...] - moved - split_product(whole, fac_mix[...]), inv_lo[...])
    out_mix[...] = mixed
    known = turned_split(inv_lo[...], turned_split(fac_mix[...], moved))
    base[...] = top_lo[...] + known - turned_split(mixed, fac_mix[...])


def last_kernel(inner, inv, fac, base, result):
    turned = inv[...].T
    lower = jnp.tril(base[...] - split_product(turned, inner[...]))
    middle = lower_half(turned_split(fac[...], lower))
    whole = split_product(split_product(turned, middle), inv[...])
    result[...] = lower_half(whole + whole.T)


def pack_kernel(at_ref, first_ref, second_ref, stay_ref, go_ref):
    stay_ref[0] = first_ref[...]
    go_ref[0] = second_ref[...]


def pack_panel(panel, after=()):
    width, owned = panel.shape
    owners = lax.axis_size("col")
    part = owned // owners
    here = lax.axis_index("col")
    if part % CB:
        blocks = panel.reshape(width, owners, part).transpose(1, 0, 2)
        blocks = jnp.take(blocks, jnp.arange(owners) ^ here, axis=0)
        return blocks[0::2], blocks[1::2]
    shape = jax.ShapeDtypeStruct((owners // 2, width, part), jnp.float32)
    out_spec = pl.BlockSpec((1, width, part), lambda j, at: (j, 0, 0))
    return pl.pallas_call(
        pack_kernel,
        out_shape=(shape, shape),
        grid_spec=pltpu.PrefetchScalarGridSpec(
            num_scalar_prefetch=1,
            grid=(owners // 2,),
            in_specs=[
                pl.BlockSpec((width, part), lambda j, at: (0, (2 * j) ^ at[0])),
                pl.BlockSpec((width, part), lambda j, at: (0, (2 * j + 1) ^ at[0])),
            ],
            out_specs=(out_spec, out_spec),
        ),
        compiler_params=pltpu.CompilerParams(vmem_limit_bytes=VMEM_LIMIT),
        cost_estimate=cost(8 * 256 * panel.size),
    )(jnp.full((1,), here, jnp.int32), panel, panel)


def regroup_kernel(tile, at_ref, *refs):
    pairs, out_ref, blocks_ref = refs[:-2], refs[-2], refs[-1]
    owners, _, part = blocks_ref.shape
    rows = out_ref.shape[0]
    for j, pair in enumerate(pairs):
        blocks_ref[2 * j] = pair[0]
        blocks_ref[2 * j + 1] = pair[1]
    for offset in range(rows):
        lane = 0
        for q in range(0, part, tile):
            for group in range(owners // rows):
                source = (at_ref[0] ^ offset) + rows * (group ^ at_ref[1])
                out_ref[offset, :, lane : lane + tile] = blocks_ref[source, :, q : q + tile]
                lane += tile


def place_kernel(at_ref, *refs):
    pieces, out_ref = refs[:-1], refs[-1]
    for offset, piece in enumerate(pieces):
        out_ref[at_ref[0] ^ offset] = piece[...]


def align_rows(pairs, after):
    width, part = pairs[0].shape[1:]
    owners = 2 * len(pairs)
    row_owners = lax.axis_size("row")
    here = lax.axis_index("col")
    row = lax.axis_index("row")
    rows = part * owners // row_owners
    at = jnp.stack([(here % row_owners) ^ row, here // row_owners]).astype(jnp.int32)
    grouped = whole_in_vmem(
        functools.partial(regroup_kernel, min(CB, part)),
        jax.ShapeDtypeStruct((row_owners, width, rows), jnp.float32),
        [pltpu.VMEM((owners, width, part), jnp.float32)],
        pairs,
        4 * 256 * owners * width * part,
        scalars=at,
        after=after,
    )
    arrived = [grouped[0]]
    arrived += [swap(grouped[offset], "row", offset) for offset in range(1, row_owners)]
    return arrived, grouped


def place_rows(arrived, after):
    row_owners = len(arrived)
    width, rows = arrived[0].shape
    aligned = whole_in_vmem(
        place_kernel,
        jax.ShapeDtypeStruct((row_owners, width, rows), jnp.float32),
        [],
        arrived,
        1024,
        scalars=jnp.full((1,), lax.axis_index("row"), jnp.int32),
        after=after,
    )
    return aligned.reshape(row_owners * width, rows)


def turn_kernel(source, target):
    turned = source[...].T
    chunk = target.shape[1]
    for at in range(target.shape[0]):
        target[at] = turned[at * chunk : (at + 1) * chunk]


def settle_kernel(at_ref, summed, grads, aligned, rest_out, inner_out):
    rest = grads[at_ref[0]] - 2.0 * summed[...]
    rest_out[...] = rest
    inner_out[...] = dims_dot(rest, aligned[...], 1, 1)


def adjoint_kernel(at_ref, inverse, *refs):
    total = 0.0
    for slot, rest in enumerate(refs[:-1]):
        total += turned_split(rest[...], inverse[at_ref[slot]])
    refs[-1][...] = total


def neighbour_panels(panel):
    bits = lax.axis_size("row").bit_length() - 1
    return {0: [panel]} | {1 << b: [swap(panel, "row", 1 << b)] for b in range(bits)}


def copy_kernel(source, target):
    target[...] = source[...]


def stage_kernel(panel, stay, arrived, later, *pairs):
    later[...] = panel[...]
    for j, pair in enumerate(pairs):
        pair[0] = stay[j]
        pair[1] = arrived[j]


def stage(panel, stay, arrived, after):
    shapes = [jax.ShapeDtypeStruct(panel.shape, jnp.float32)]
    shapes += [jax.ShapeDtypeStruct((2,) + stay.shape[1:], jnp.float32)] * stay.shape[0]
    later, *pairs = whole_in_vmem(
        stage_kernel, shapes, [], [panel, stay, arrived], 8 * 256 * panel.size, after=after
    )
    return later, pairs


def times_trail_kernel(offsets, counts, at_ref, *refs):
    panel_refs, trail_ref = refs[: sum(counts)], refs[sum(counts)]
    out_ref, panel_at, halves_at = refs[-3:]

    @pl.when(pl.program_id(0) == 0)
    def _():
        first = 0
        for offset, count in zip(offsets, counts):
            pieces = panel_refs[first : first + count]
            first += count

            @pl.when(at_ref[0] == offset)
            def _():
                row = 0
                for piece in pieces:
                    panel_at[row : row + piece.shape[0]] = piece[...]
                    row += piece.shape[0]

        panel = panel_at[...]
        high = panel.astype(jnp.bfloat16)
        halves_at[: panel.shape[0]] = high
        halves_at[panel.shape[0] :] = (panel - high.astype(jnp.float32)).astype(jnp.bfloat16)

    width = panel_at.shape[0]
    depth = trail_ref.shape[1]
    step = min(depth, 2 * NB)
    total = jnp.zeros(out_ref.shape[1:], jnp.float32)
    for k in range(0, depth, step):
        trail = trail_ref[:, k : k + step]
        high = trail.astype(jnp.bfloat16)
        low = (trail - high.astype(jnp.float32)).astype(jnp.bfloat16)
        both = dims_dot(halves_at[:, k : k + step], high, 1, 1, None)
        total += both[:width] + both[width:]
        total += dims_dot(halves_at[:width, k : k + step], low, 1, 1, None)
    out_ref[0] = total


def times_trail(candidates, offset, core, trail, weight, after=()):
    offsets = tuple(candidates)
    counts = tuple(len(candidates[each]) for each in offsets)
    pieces = [piece for each in offsets for piece in candidates[each]]
    width = sum(piece.shape[0] for piece in candidates[offsets[0]])
    depth = trail.shape[1]
    planes = lax.axis_size("col") // 2
    rows = trail.shape[0] // (2 * planes)
    at = jnp.stack([offset, core]).astype(jnp.int32)
    return pl.pallas_call(
        functools.partial(times_trail_kernel, offsets, counts),
        out_shape=jax.ShapeDtypeStruct((planes, width, rows), jnp.float32),
        grid_spec=pltpu.PrefetchScalarGridSpec(
            num_scalar_prefetch=1,
            grid=(planes,),
            in_specs=[pl.BlockSpec(piece.shape, lambda j, at: (0, 0)) for piece in pieces]
            + [pl.BlockSpec((rows, depth), lambda j, at: (2 * j + at[1], 0))]
            + [pl.BlockSpec(memory_space=pl.ANY)] * len(after),
            out_specs=pl.BlockSpec((1, width, rows), lambda j, at: (j, 0, 0)),
            scratch_shapes=[
                pltpu.VMEM((width, depth), jnp.float32),
                pltpu.VMEM((2 * width, depth), jnp.bfloat16),
            ],
        ),
        compiler_params=pltpu.CompilerParams(vmem_limit_bytes=VMEM_LIMIT),
        cost_estimate=cost(weight * 8.6 * width * depth * rows * planes),
    )(at, *pieces, trail, *after)


def sum_over_planes(block):
    planes, width, rows = block.shape
    groups = [[2 * plane + core for plane in range(planes)] for core in range(2)]
    return lax.psum_scatter(
        block.reshape(planes * width, rows),
        "col",
        scatter_dimension=0,
        tiled=True,
        axis_index_groups=groups,
    )


def pick(blocks, which):
    return lax.dynamic_index_in_dim(blocks, which, 0, keepdims=False)


def swap(block, axis, offset):
    return lax.ppermute(block, axis, [(i, i ^ offset) for i in range(lax.axis_size(axis))])


def exchange_order():
    order = [("col", 1)]
    order += [("row", 1 << b) for b in range(lax.axis_size("row").bit_length() - 1)]
    order += [("col", 1 << b) for b in range(1, lax.axis_size("col").bit_length() - 1)]
    return order


def sum_shares(block, least, order, halved=()):
    halved = list(halved)
    for axis, bit in order:
        rows = block.shape[0]
        if rows // 2 >= least and rows % 16 == 0:
            upper = (lax.axis_index(axis) & bit) != 0
            low, high = block[: rows // 2], block[rows // 2 :]
            block = jnp.where(upper, high, low) + swap(jnp.where(upper, low, high), axis, bit)
            halved.append((axis, bit, upper))
        else:
            block = block + swap(block, axis, bit)
    return block, halved


def join_shares(block, halved):
    for axis, bit, upper in reversed(halved):
        other = swap(block, axis, bit)
        block = jnp.concatenate([jnp.where(upper, other, block), jnp.where(upper, block, other)], 0)
    return block


def slot_table(row_owners):
    table = []
    for row in range(row_owners):
        rest = [row ^ (1 << b) for b in range(row_owners.bit_length() - 1)]
        second = max(rest)
        others = [c for c in range(row_owners - 1, -1, -1) if c not in (row, second)]
        table.append([row, second] + others)
    return np.array(table)


def per_device(trail_grad, factor_rows, factor_top, rows_grad, top_grad):
    row_owner = lax.axis_index("row")
    row_owners = lax.axis_size("row")
    core = lax.axis_index("col") % 2
    panel_width = factor_top.shape[0]
    chunk = factor_rows.shape[1]
    own_rows = rows_grad.shape[0]
    table = slot_table(row_owners)
    late = len(set(table[:, -1]))
    split = late * chunk
    whiches = [jnp.asarray(table[:, slot])[row_owner] for slot in range(row_owners)]

    own_panel = factor_rows.T
    stay, go = pack_panel(own_panel)
    arrived = swap(go, "col", 1)
    panels = neighbour_panels(own_panel)

    aligned = None

    def multiply(slot, after):
        nonlocal aligned
        offset = whiches[slot] ^ row_owner
        offsets = sorted({int(table[r, slot]) ^ r for r in range(row_owners)})
        candidates = {each: panels[each] for each in offsets}
        theirs = times_trail(candidates, offset, 1 - core, trail_grad, WEIGHTS[min(slot, 2)], after)
        between = (ahead,) if slot == 0 else ()
        if slot == row_owners - 1:
            aligned = place_rows(spread, (theirs,))
            between = (aligned,)
        ours = times_trail(
            candidates, offset, core, trail_grad, WEIGHTS[min(slot, 2)], (theirs, *between)
        )
        half = theirs.shape[0] // 2
        if slot == 1 and half:
            theirs = [swap(theirs[:half], "col", 1), swap(theirs[half:], "col", 1)]
            theirs = jnp.concatenate(theirs, 0)
        else:
            theirs = swap(theirs, "col", 1)
        total = ours + theirs
        return sum_over_planes(total), total

    def settle(slot, after=()):
        shapes = [
            jax.ShapeDtypeStruct((chunk, own_rows), jnp.float32),
            jax.ShapeDtypeStruct((chunk, panel_width), jnp.float32),
        ]
        return whole_in_vmem(
            settle_kernel,
            shapes,
            [],
            [waiting[slot], grads, aligned],
            1024,
            scalars=jnp.full((1,), whiches[slot], jnp.int32),
            after=after,
        )

    planes = stay.shape[0]
    first = planes // 2
    ahead = swap(jnp.stack([stay[first], arrived[first]]), "col", 2 * first)
    summed, done = multiply(0, (arrived,))
    waiting = [summed]
    near = [panels[offset][0] for offset in panels if offset]
    later, pairs = stage(own_panel, stay, arrived, (done, *near))
    for offset in range(1, row_owners):
        if offset not in panels:
            panels[offset] = [swap(later, "row", offset)]
    pairs = [
        pairs[0] if j == 0 else ahead if j == first else swap(pairs[j], "col", 2 * j)
        for j in range(planes)
    ]
    done = later
    for slot in range(1, row_owners):
        if slot == 2:
            inverse = triangular_inverse(factor_top, (done,))
            grads = done = whole_in_vmem(
                turn_kernel,
                jax.ShapeDtypeStruct((row_owners, chunk, own_rows), jnp.float32),
                [],
                [rows_grad],
                1024,
                after=(inverse,),
            )
        if slot == row_owners - 1:
            spread, done = align_rows(pairs, (done, waiting[0]))
        before = (waiting[slot - 2],) if slot >= 3 else ()
        summed, done = multiply(slot, (done, *before))
        waiting.append(summed)
    rests, inner = [], []
    for slot in range(row_owners - 1):
        rest, part = settle(slot, (done,))
        done = part
        rests.append(rest)
        inner.append(part)
    early = jnp.concatenate(
        [
            sum(jnp.where(whiches[s] == each, inner[s], 0.0) for s in range(row_owners - 1))
            for each in range(late, row_owners)
        ],
        0,
    )
    order = exchange_order()
    share, halved = sum_shares(early, 8, order[:STEPS])
    rest, part = settle(row_owners - 1)
    rests.append(rest)
    share = whole_in_vmem(
        copy_kernel,
        jax.ShapeDtypeStruct(share.shape, jnp.float32),
        [],
        [share],
        1024,
        after=(part,),
    )
    early = join_shares(*sum_shares(share, 8, order[STEPS:], halved))
    inner.append(part)
    adjoint = whole_in_vmem(
        adjoint_kernel,
        jax.ShapeDtypeStruct((own_rows, panel_width), jnp.float32),
        [],
        [inverse.reshape(row_owners, chunk, panel_width), *rests],
        24 * own_rows * panel_width**2,
        scalars=jnp.stack(whiches).astype(jnp.int32),
    )
    last = jnp.concatenate(
        [
            sum(jnp.where(whiches[s] == each, inner[s][:, :split], 0.0) for s in range(row_owners))
            for each in range(late)
        ],
        0,
    )
    last = join_shares(*sum_shares(last, 64, order))

    lo, hi = slice(0, split), slice(split, panel_width)
    rest = panel_width - split
    out_hi, out_mix, base = whole_in_vmem(
        early_kernel,
        [jax.ShapeDtypeStruct(each, jnp.float32) for each in ((rest, rest), (rest, split), (split, split))],
        [],
        [
            early,
            inverse[hi, hi],
            inverse[lo, lo],
            factor_top[hi, hi],
            factor_top[hi, lo],
            top_grad[hi, hi],
            top_grad[hi, lo],
            top_grad[lo, lo],
        ],
        36 * panel_width**3,
    )
    out_lo = whole_in_vmem(
        last_kernel,
        jax.ShapeDtypeStruct((split, split), jnp.float32),
        [],
        [last, inverse[lo, lo], factor_top[lo, lo], base],
        14 * panel_width**3,
    )
    top_out = jnp.concatenate(
        [
            jnp.concatenate([out_lo, jnp.zeros((split, rest), jnp.float32)], 1),
            jnp.concatenate([out_mix, out_hi], 1),
        ],
        0,
    )
    return adjoint, top_out


def solution(mesh):
    placed = (P("row", "col"), P("col", "row"), P(), P(("row", "col"), None), P())
    return jax.shard_map(
        per_device,
        mesh=mesh,
        in_specs=placed,
        out_specs=(P(("row", "col"), None), P()),
        check_vma=False,
    )
```

```python
import functools

import jax
import jax.numpy as jnp
import numpy as np
from jax import lax
from jax.experimental import pallas as pl
from jax.experimental.pallas import tpu as pltpu
from jax.sharding import PartitionSpec as P

NB = 256
NP = 3
CB = 128
LEAF = 32
STEPS = 2
VMEM_LIMIT = 48 * 1024 * 1024
WEIGHTS = (4.0, 0.4, 2.0)

exact_dots = lax.Precision.HIGHEST
split_dots = lax.Precision.HIGH


def dims_dot(left, right, left_dim, right_dim, precision=exact_dots):
    return lax.dot_general(
        left,
        right,
        (((left_dim,), (right_dim,)), ((), ())),
        precision=precision,
        preferred_element_type=jnp.float32,
    )


def product(left, right):
    return dims_dot(left, right, 1, 0)


def lower_half(matrix):
    row_ids = lax.broadcasted_iota(jnp.int32, matrix.shape, 0)
    col_ids = lax.broadcasted_iota(jnp.int32, matrix.shape, 1)
    return jnp.where(row_ids > col_ids, matrix, jnp.where(row_ids == col_ids, 0.5 * matrix, 0.0))


def inverse_kernel(factor_ref, out_ref, spread_ref, leaf_out):
    width = factor_ref.shape[0]
    dot = functools.partial(jnp.dot, precision=exact_dots, preferred_element_type=jnp.float32)
    rows = lax.broadcasted_iota(jnp.int32, (CB, CB), 0)
    cols = lax.broadcasted_iota(jnp.int32, (CB, CB), 1)
    same_leaf = rows // LEAF == cols // LEAF
    ones = jnp.where(same_leaf, 1.0, 0.0)
    lane_at = lax.broadcasted_iota(jnp.int32, (LEAF, CB), 1) % LEAF
    for at in range(0, width, CB):
        turned = jnp.where(same_leaf, factor_ref[at : at + CB, at : at + CB], 0.0).T
        leaves = sum(turned[low : low + LEAF] for low in range(0, CB, LEAF))
        picked = jnp.concatenate(
            [jnp.where(lane_at == row, leaves, 0.0) for row in range(LEAF)], 0
        )
        spread_ref[:, at : at + CB] = dot(picked, ones)
    lane = lax.broadcasted_iota(jnp.int32, (1, width), 1) % LEAF
    row_at = lax.broadcasted_iota(jnp.int32, (LEAF, width), 0)
    leaf_out[...] = jnp.zeros_like(leaf_out)
    for row in range(LEAF):
        known = spread_ref[row * LEAF : (row + 1) * LEAF]
        diag = known[row : row + 1]
        total = jnp.sum(jnp.where(row_at < row, known * leaf_out[...], 0.0), axis=0, keepdims=True)
        leaf_out[row : row + 1] = (jnp.where(lane == row, 1.0, 0.0) - total) / diag
    out_ref[...] = jnp.zeros_like(out_ref)
    for at in range(0, width, CB):
        spread = jnp.concatenate([leaf_out[:, at : at + CB]] * (CB // LEAF), 0)
        inv = jnp.where(same_leaf, spread, 0.0)
        block = factor_ref[at : at + CB, at : at + CB]
        size = LEAF
        while size < CB:
            below = (rows // size == cols // size + 1) & (rows // (2 * size) == cols // (2 * size))
            inv = inv - dot(dot(inv, jnp.where(below, block, 0.0)), inv)
            size *= 2
        out_ref[at : at + CB, at : at + CB] = inv
    for at in range(0, width, NB):
        size = CB
        while size < NB:
            for low in range(at, at + NB, 2 * size):
                mid, high = low + size, low + 2 * size
                first = out_ref[low:mid, low:mid]
                second = out_ref[mid:high, mid:high]
                out_ref[mid:high, low:mid] = -dot(dot(second, factor_ref[mid:high, low:mid]), first)
            size *= 2
    for at in range(NB, width, NB):
        carried = dot(factor_ref[at : at + NB, :at], out_ref[:at, :at])
        out_ref[at : at + NB, :at] = -dot(out_ref[at : at + NB, at : at + NB], carried)


def cost(flops):
    return pl.CostEstimate(flops=int(flops), bytes_accessed=1024, transcendentals=0)


def whole_in_vmem(kernel, out_shape, scratch, operands, flops, scalars=None, after=()):
    first = () if scalars is None else (scalars,)

    def body(*refs):
        head = refs[: len(first)]
        inputs = refs[len(first) : len(first) + len(operands)]
        rest = refs[len(first) + len(operands) + len(after) :]
        kernel(*head, *inputs, *rest)

    return pl.pallas_call(
        body,
        out_shape=out_shape,
        in_specs=[pl.BlockSpec(memory_space=pltpu.SMEM)] * len(first)
        + [pl.BlockSpec(memory_space=pltpu.VMEM)] * len(operands)
        + [pl.BlockSpec(memory_space=pl.ANY)] * len(after),
        out_specs=jax.tree.map(lambda _: pl.BlockSpec(memory_space=pltpu.VMEM), out_shape),
        scratch_shapes=scratch,
        compiler_params=pltpu.CompilerParams(vmem_limit_bytes=VMEM_LIMIT),
        cost_estimate=cost(flops),
    )(*first, *operands, *after)


def triangular_inverse(factor, after):
    width = factor.shape[0]
    return whole_in_vmem(
        inverse_kernel,
        jax.ShapeDtypeStruct((width, width), jnp.float32),
        [pltpu.VMEM((LEAF * LEAF, width), jnp.float32), pltpu.VMEM((LEAF, width), jnp.float32)],
        [factor],
        1024,
        after=after,
    )


def halves(matrix):
    high = matrix.astype(jnp.bfloat16)
    return high, (matrix - high.astype(jnp.float32)).astype(jnp.bfloat16)


def split_product(left, right):
    left_high, left_low = halves(left)
    right_high, right_low = halves(right)
    small = dims_dot(left_low, right_high, 1, 0, None) + dims_dot(left_high, right_low, 1, 0, None)
    return dims_dot(left_high, right_high, 1, 0, None) + small


def turned_split(left, right):
    return split_product(left.T, right)


def early_kernel(inner, inv_hi, inv_lo, fac_hi, fac_mix, top_hi, top_mix, top_lo, out_hi, out_mix, base):
    split = inv_lo.shape[0]
    turned = inv_hi[...].T
    moved = split_product(turned, inner[...])
    lower = jnp.tril(top_hi[...] - moved[:, split:])
    middle = lower_half(turned_split(fac_hi[...], lower))
    whole = split_product(split_product(turned, middle), inv_hi[...])
    whole = whole + whole.T
    out_hi[...] = lower_half(whole)
    moved = moved[:, :split]
    mixed = split_product(top_mix[...] - moved - split_product(whole, fac_mix[...]), inv_lo[...])
    out_mix[...] = mixed
    known = turned_split(inv_lo[...], turned_split(fac_mix[...], moved))
    base[...] = top_lo[...] + known - turned_split(mixed, fac_mix[...])


def last_kernel(inner, inv, fac, base, result):
    turned = inv[...].T
    lower = jnp.tril(base[...] - split_product(turned, inner[...]))
    middle = lower_half(turned_split(fac[...], lower))
    whole = split_product(split_product(turned, middle), inv[...])
    result[...] = lower_half(whole + whole.T)


def pack_kernel(at_ref, first_ref, second_ref, stay_ref, go_ref):
    stay_ref[0] = first_ref[...]
    go_ref[0] = second_ref[...]


def pack_panel(panel, after=()):
    width, owned = panel.shape
    owners = lax.axis_size("col")
    part = owned // owners
    here = lax.axis_index("col")
    if part % CB:
        blocks = panel.reshape(width, owners, part).transpose(1, 0, 2)
        blocks = jnp.take(blocks, jnp.arange(owners) ^ here, axis=0)
        return blocks[0::2], blocks[1::2]
    shape = jax.ShapeDtypeStruct((owners // 2, width, part), jnp.float32)
    out_spec = pl.BlockSpec((1, width, part), lambda j, at: (j, 0, 0))
    return pl.pallas_call(
        pack_kernel,
        out_shape=(shape, shape),
        grid_spec=pltpu.PrefetchScalarGridSpec(
            num_scalar_prefetch=1,
            grid=(owners // 2,),
            in_specs=[
                pl.BlockSpec((width, part), lambda j, at: (0, (2 * j) ^ at[0])),
                pl.BlockSpec((width, part), lambda j, at: (0, (2 * j + 1) ^ at[0])),
            ],
            out_specs=(out_spec, out_spec),
        ),
        compiler_params=pltpu.CompilerParams(vmem_limit_bytes=VMEM_LIMIT),
        cost_estimate=cost(8 * 256 * panel.size),
    )(jnp.full((1,), here, jnp.int32), panel, panel)


def regroup_kernel(tile, at_ref, *refs):
    pairs, out_ref, blocks_ref = refs[:-2], refs[-2], refs[-1]
    owners, _, part = blocks_ref.shape
    rows = out_ref.shape[0]
    for j, pair in enumerate(pairs):
        blocks_ref[2 * j] = pair[0]
        blocks_ref[2 * j + 1] = pair[1]
    for offset in range(rows):
        lane = 0
        for q in range(0, part, tile):
            for group in range(owners // rows):
                source = (at_ref[0] ^ offset) + rows * (group ^ at_ref[1])
                out_ref[offset, :, lane : lane + tile] = blocks_ref[source, :, q : q + tile]
                lane += tile


def place_kernel(at_ref, *refs):
    pieces, out_ref = refs[:-1], refs[-1]
    for offset, piece in enumerate(pieces):
        out_ref[at_ref[0] ^ offset] = piece[...]


def align_rows(pairs, after):
    width, part = pairs[0].shape[1:]
    owners = 2 * len(pairs)
    row_owners = lax.axis_size("row")
    here = lax.axis_index("col")
    row = lax.axis_index("row")
    rows = part * owners // row_owners
    at = jnp.stack([(here % row_owners) ^ row, here // row_owners]).astype(jnp.int32)
    grouped = whole_in_vmem(
        functools.partial(regroup_kernel, min(CB, part)),
        jax.ShapeDtypeStruct((row_owners, width, rows), jnp.float32),
        [pltpu.VMEM((owners, width, part), jnp.float32)],
        pairs,
        4 * 256 * owners * width * part,
        scalars=at,
        after=after,
    )
    arrived = [grouped[0]]
    arrived += [swap(grouped[offset], "row", offset) for offset in range(1, row_owners)]
    return arrived, grouped


def place_rows(arrived, after):
    row_owners = len(arrived)
    width, rows = arrived[0].shape
    aligned = whole_in_vmem(
        place_kernel,
        jax.ShapeDtypeStruct((row_owners, width, rows), jnp.float32),
        [],
        arrived,
        1024,
        scalars=jnp.full((1,), lax.axis_index("row"), jnp.int32),
        after=after,
    )
    return aligned.reshape(row_owners * width, rows)


def turn_kernel(source, target):
    turned = source[...].T
    chunk = target.shape[1]
    for at in range(target.shape[0]):
        target[at] = turned[at * chunk : (at + 1) * chunk]


def settle_kernel(at_ref, summed, grads, aligned, rest_out, inner_out):
    rest = grads[at_ref[0]] - 2.0 * summed[...]
    rest_out[...] = rest
    inner_out[...] = dims_dot(rest, aligned[...], 1, 1)


def adjoint_kernel(at_ref, inverse, *refs):
    total = 0.0
    for slot, rest in enumerate(refs[:-1]):
        total += turned_split(rest[...], inverse[at_ref[slot]])
    refs[-1][...] = total


def neighbour_panels(panel):
    bits = lax.axis_size("row").bit_length() - 1
    return {0: [panel]} | {1 << b: [swap(panel, "row", 1 << b)] for b in range(bits)}


def copy_kernel(source, target):
    target[...] = source[...]


def stage_kernel(panel, stay, arrived, later, *pairs):
    later[...] = panel[...]
    for j, pair in enumerate(pairs):
        pair[0] = stay[j]
        pair[1] = arrived[j]


def stage(panel, stay, arrived, after):
    shapes = [jax.ShapeDtypeStruct(panel.shape, jnp.float32)]
    shapes += [jax.ShapeDtypeStruct((2,) + stay.shape[1:], jnp.float32)] * stay.shape[0]
    later, *pairs = whole_in_vmem(
        stage_kernel, shapes, [], [panel, stay, arrived], 8 * 256 * panel.size, after=after
    )
    return later, pairs


def times_trail_kernel(offsets, counts, at_ref, *refs):
    panel_refs, trail_ref = refs[: sum(counts)], refs[sum(counts)]
    out_ref, panel_at, halves_at = refs[-3:]

    @pl.when(pl.program_id(0) == 0)
    def _():
        first = 0
        for offset, count in zip(offsets, counts):
            pieces = panel_refs[first : first + count]
            first += count

            @pl.when(at_ref[0] == offset)
            def _():
                row = 0
                for piece in pieces:
                    panel_at[row : row + piece.shape[0]] = piece[...]
                    row += piece.shape[0]

        panel = panel_at[...]
        high = panel.astype(jnp.bfloat16)
        halves_at[: panel.shape[0]] = high
        halves_at[panel.shape[0] :] = (panel - high.astype(jnp.float32)).astype(jnp.bfloat16)

    width = panel_at.shape[0]
    depth = trail_ref.shape[1]
    step = min(depth, 2 * NB)
    total = jnp.zeros(out_ref.shape[1:], jnp.float32)
    for k in range(0, depth, step):
        trail = trail_ref[:, k : k + step]
        high = trail.astype(jnp.bfloat16)
        low = (trail - high.astype(jnp.float32)).astype(jnp.bfloat16)
        both = dims_dot(halves_at[:, k : k + step], high, 1, 1, None)
        total += both[:width] + both[width:]
        total += dims_dot(halves_at[:width, k : k + step], low, 1, 1, None)
    out_ref[0] = total


def times_trail(candidates, offset, core, trail, weight, after=()):
    offsets = tuple(candidates)
    counts = tuple(len(candidates[each]) for each in offsets)
    pieces = [piece for each in offsets for piece in candidates[each]]
    width = sum(piece.shape[0] for piece in candidates[offsets[0]])
    depth = trail.shape[1]
    planes = lax.axis_size("col") // 2
    rows = trail.shape[0] // (2 * planes)
    at = jnp.stack([offset, core]).astype(jnp.int32)
    return pl.pallas_call(
        functools.partial(times_trail_kernel, offsets, counts),
        out_shape=jax.ShapeDtypeStruct((planes, width, rows), jnp.float32),
        grid_spec=pltpu.PrefetchScalarGridSpec(
            num_scalar_prefetch=1,
            grid=(planes,),
            in_specs=[pl.BlockSpec(piece.shape, lambda j, at: (0, 0)) for piece in pieces]
            + [pl.BlockSpec((rows, depth), lambda j, at: (2 * j + at[1], 0))]
            + [pl.BlockSpec(memory_space=pl.ANY)] * len(after),
            out_specs=pl.BlockSpec((1, width, rows), lambda j, at: (j, 0, 0)),
            scratch_shapes=[
                pltpu.VMEM((width, depth), jnp.float32),
                pltpu.VMEM((2 * width, depth), jnp.bfloat16),
            ],
        ),
        compiler_params=pltpu.CompilerParams(vmem_limit_bytes=VMEM_LIMIT),
        cost_estimate=cost(weight * 8.6 * width * depth * rows * planes),
    )(at, *pieces, trail, *after)


def sum_over_planes(block):
    planes, width, rows = block.shape
    groups = [[2 * plane + core for plane in range(planes)] for core in range(2)]
    return lax.psum_scatter(
        block.reshape(planes * width, rows),
        "col",
        scatter_dimension=0,
        tiled=True,
        axis_index_groups=groups,
    )


def pick(blocks, which):
    return lax.dynamic_index_in_dim(blocks, which, 0, keepdims=False)


def swap(block, axis, offset):
    return lax.ppermute(block, axis, [(i, i ^ offset) for i in range(lax.axis_size(axis))])


def exchange_order():
    order = [("col", 1)]
    order += [("row", 1 << b) for b in range(lax.axis_size("row").bit_length() - 1)]
    order += [("col", 1 << b) for b in range(1, lax.axis_size("col").bit_length() - 1)]
    return order


def sum_shares(block, least, order, halved=()):
    halved = list(halved)
    for axis, bit in order:
        rows = block.shape[0]
        if rows // 2 >= least and rows % 16 == 0:
            upper = (lax.axis_index(axis) & bit) != 0
            low, high = block[: rows // 2], block[rows // 2 :]
            block = jnp.where(upper, high, low) + swap(jnp.where(upper, low, high), axis, bit)
            halved.append((axis, bit, upper))
        else:
            block = block + swap(block, axis, bit)
    return block, halved


def join_shares(block, halved):
    for axis, bit, upper in reversed(halved):
        other = swap(block, axis, bit)
        block = jnp.concatenate([jnp.where(upper, other, block), jnp.where(upper, block, other)], 0)
    return block


def slot_table(row_owners):
    table = []
    for row in range(row_owners):
        rest = [row ^ (1 << b) for b in range(row_owners.bit_length() - 1)]
        second = max(rest)
        others = [c for c in range(row_owners - 1, -1, -1) if c not in (row, second)]
        table.append([row, second] + others)
    return np.array(table)


def per_device(trail_grad, factor_rows, factor_top, rows_grad, top_grad):
    row_owner = lax.axis_index("row")
    row_owners = lax.axis_size("row")
    core = lax.axis_index("col") % 2
    panel_width = factor_top.shape[0]
    chunk = factor_rows.shape[1]
    own_rows = rows_grad.shape[0]
    table = slot_table(row_owners)
    late = len(set(table[:, -1]))
    split = late * chunk
    whiches = [jnp.asarray(table[:, slot])[row_owner] for slot in range(row_owners)]

    own_panel = factor_rows.T
    stay, go = pack_panel(own_panel)
    arrived = swap(go, "col", 1)
    panels = neighbour_panels(own_panel)

    aligned = None

    def multiply(slot, after):
        nonlocal aligned
        offset = whiches[slot] ^ row_owner
        offsets = sorted({int(table[r, slot]) ^ r for r in range(row_owners)})
        candidates = {each: panels[each] for each in offsets}
        theirs = times_trail(candidates, offset, 1 - core, trail_grad, WEIGHTS[min(slot, 2)], after)
        between = (ahead,) if slot == 0 else ()
        if slot == row_owners - 1:
            aligned = place_rows(spread, (theirs,))
            between = (aligned,)
        ours = times_trail(
            candidates, offset, core, trail_grad, WEIGHTS[min(slot, 2)], (theirs, *between)
        )
        half = theirs.shape[0] // 2
        if slot == 1 and half:
            theirs = [swap(theirs[:half], "col", 1), swap(theirs[half:], "col", 1)]
            theirs = jnp.concatenate(theirs, 0)
        else:
            theirs = swap(theirs, "col", 1)
        total = ours + theirs
        return sum_over_planes(total), total

    def settle(slot, after=()):
        shapes = [
            jax.ShapeDtypeStruct((chunk, own_rows), jnp.float32),
            jax.ShapeDtypeStruct((chunk, panel_width), jnp.float32),
        ]
        return whole_in_vmem(
            settle_kernel,
            shapes,
            [],
            [waiting[slot], grads, aligned],
            1024,
            scalars=jnp.full((1,), whiches[slot], jnp.int32),
            after=after,
        )

    planes = stay.shape[0]
    first = planes // 2
    ahead = swap(jnp.stack([stay[first], arrived[first]]), "col", 2 * first)
    summed, done = multiply(0, (arrived,))
    waiting = [summed]
    near = [panels[offset][0] for offset in panels if offset]
    later, pairs = stage(own_panel, stay, arrived, (done, *near))
    for offset in range(1, row_owners):
        if offset not in panels:
            panels[offset] = [swap(later, "row", offset)]
    pairs = [
        pairs[0] if j == 0 else ahead if j == first else swap(pairs[j], "col", 2 * j)
        for j in range(planes)
    ]
    done = later
    for slot in range(1, row_owners):
        if slot == 2:
            inverse = triangular_inverse(factor_top, (done,))
            grads = done = whole_in_vmem(
                turn_kernel,
                jax.ShapeDtypeStruct((row_owners, chunk, own_rows), jnp.float32),
                [],
                [rows_grad],
                1024,
                after=(inverse,),
            )
        if slot == row_owners - 1:
            spread, done = align_rows(pairs, (done, waiting[0]))
        before = (waiting[slot - 2],) if slot >= 3 else ()
        summed, done = multiply(slot, (done, *before))
        waiting.append(summed)
    rests, inner = [], []
    for slot in range(row_owners - 1):
        rest, part = settle(slot, (done,))
        done = part
        rests.append(rest)
        inner.append(part)
    early = jnp.concatenate(
        [
            sum(jnp.where(whiches[s] == each, inner[s], 0.0) for s in range(row_owners - 1))
            for each in range(late, row_owners)
        ],
        0,
    )
    order = exchange_order()
    share, halved = sum_shares(early, 8, order[:STEPS])
    rest, part = settle(row_owners - 1)
    rests.append(rest)
    share = whole_in_vmem(
        copy_kernel,
        jax.ShapeDtypeStruct(share.shape, jnp.float32),
        [],
        [share],
        1024,
        after=(part,),
    )
    early = join_shares(*sum_shares(share, 8, order[STEPS:], halved))
    inner.append(part)
    adjoint = whole_in_vmem(
        adjoint_kernel,
        jax.ShapeDtypeStruct((own_rows, panel_width), jnp.float32),
        [],
        [inverse.reshape(row_owners, chunk, panel_width), *rests],
        24 * own_rows * panel_width**2,
        scalars=jnp.stack(whiches).astype(jnp.int32),
    )
    last = jnp.concatenate(
        [
            sum(jnp.where(whiches[s] == each, inner[s][:, :split], 0.0) for s in range(row_owners))
            for each in range(late)
        ],
        0,
    )
    last = join_shares(*sum_shares(last, 64, order))

    lo, hi = slice(0, split), slice(split, panel_width)
    rest = panel_width - split
    out_hi, out_mix, base = whole_in_vmem(
        early_kernel,
        [jax.ShapeDtypeStruct(each, jnp.float32) for each in ((rest, rest), (rest, split), (split, split))],
        [],
        [
            early,
            inverse[hi, hi],
            inverse[lo, lo],
            factor_top[hi, hi],
            factor_top[hi, lo],
            top_grad[hi, hi],
            top_grad[hi, lo],
            top_grad[lo, lo],
        ],
        36 * panel_width**3,
    )
    out_lo = whole_in_vmem(
        last_kernel,
        jax.ShapeDtypeStruct((split, split), jnp.float32),
        [],
        [last, inverse[lo, lo], factor_top[lo, lo], base],
        14 * panel_width**3,
    )
    top_out = jnp.concatenate(
        [
            jnp.concatenate([out_lo, jnp.zeros((split, rest), jnp.float32)], 1),
            jnp.concatenate([out_mix, out_hi], 1),
        ],
        0,
    )
    return adjoint, top_out


def solution(mesh):
    placed = (P("row", "col"), P("col", "row"), P(), P(("row", "col"), None), P())
    return jax.shard_map(
        per_device,
        mesh=mesh,
        in_specs=placed,
        out_specs=(P(("row", "col"), None), P()),
        check_vma=False,
    )
```
